512 devices in a mesh: expert: 64 (over y, x, core), tensor: 8 (over z).
Axes of the slice: x: 4, y: 8, z: 8, core: 2. Of those that a mesh axis runs over, the one named last changes fastest.
Arguments:
- tokens: bfloat16 [8192, 2048], P('expert'), may hold values from -6 to 6
- cotangent: bfloat16 [8192, 2048], P('expert'), may hold values from -6 to 6
- expert_ids: int32 [8192, 8], P('expert'), may hold values from 0 to 63, all different within a row; in each aligned block of 128 rows (0 to 127, 128 to 255, ...) at most 20 rows name the same one
- gate_probs: bfloat16 [8192, 8], P('expert'), may hold values from 0.049804688 to 0.5
- w_gate: bfloat16 [64, 2048, 1024], P('expert', None, 'tensor'), may hold values from -0.125 to 0.125
- w_up: bfloat16 [64, 2048, 1024], P('expert', None, 'tensor'), may hold values from -0.125 to 0.125
- w_down: bfloat16 [64, 1024, 2048], P('expert', 'tensor'), may hold values from -0.1875 to 0.1875
Outputs:
- grad_input: bfloat16 [8192, 2048], P('expert', 'tensor')
- grad_gate: bfloat16 [64, 2048, 1024], P('expert', None, 'tensor')
- grad_up: bfloat16 [64, 2048, 1024], P('expert', None, 'tensor')
- grad_down: bfloat16 [64, 1024, 2048], P('expert', 'tensor')
The draws below stay inside these ranges and needn't reach their ends.
Inputs may be any that keep to these rules, and one draw needn't show every extreme that they name: `expert_ids`: each row names 8 different experts. In the 128 rows of one index of the expert axis no expert is named more than 20 times, a bound that some block reaches.
All inputs are finite; a program needn't handle non-finite values.
Results may differ from the reference program's by a relative error of at most 0.019.
Values may be sent and summed in bfloat16 or wider, within the bound.
A program may use at most 128 MiB of HBM per device.

```python
import math
import jax
import jax.numpy as jnp
import numpy as np
from jax import lax

D = 2048
FF = 1024
EXPERTS = 64
TOP = 8
TOK_DEV = 128
CAP = 20
TOKENS = 8192
N_EXPERT = 64
N_TENSOR = 8


def steps_of(stream_key, extent, pieces, least, largest):
    def one(position, blocks):
        draws = jax.random.uniform(jax.random.fold_in(jax.random.fold_in(stream_key, 6), position), (blocks,), jnp.float32, least / len(pieces), largest / len(pieces))
        return jnp.repeat(jnp.exp(draws), extent[position] // blocks).reshape((-1,) + (1,) * (len(extent) - position - 1))

    level = one(*pieces[0])
    for cut in pieces[1:]:
        level = level * one(*cut)
    return level


def routed_block(stream_key, own, number, rows, count, top, bound, lean):
    sequence = jax.random.permutation(stream_key, count)
    packed, usual = load_shares(count, rows * top, bound, lean, True), load_shares(count, rows * top, bound, lean, False)
    places = jnp.arange(count)

    def named(lengths, turn):
        used = int((lengths > 0).sum())
        fixed = max(1, used // 4)
        shifted = fixed + (places - fixed + turn * (used - fixed)) % max(1, count - fixed)
        return jnp.zeros((count,), jnp.int32).at[sequence[jnp.where(places < fixed, places, shifted)]].set(jnp.asarray(lengths, jnp.int32))

    lengths = jnp.where(number % 4 == 0, named(packed, number // 4), named(usual, number - number // 4 - 1))
    mixed = jax.random.permutation(jax.random.fold_in(own, 3), count)
    source_of, taker = mixed[0:count // 2 * 2:2], mixed[1:count // 2 * 2:2]
    margin = jnp.minimum(lengths[source_of] - 1, bound - lengths[taker]) // 2
    margin = jnp.where((source_of == sequence[0]) | (taker == sequence[0]) | (lengths[taker] == 0), 0, jnp.maximum(margin, 0))
    shifted = jax.random.randint(jax.random.fold_in(own, 4), (count // 2,), 0, 1 << 20) % (margin + 1)
    lengths = lengths.at[source_of].add(-shifted).at[taker].add(shifted)
    members = jnp.searchsorted(jnp.cumsum(lengths), jnp.arange(rows * top), side="right").astype(jnp.int32)
    table = members.reshape(top, rows).T
    table = table[jax.random.permutation(jax.random.fold_in(own, 1), rows)]
    turn = jax.random.randint(jax.random.fold_in(own, 2), (rows, 1), 0, top)
    return jnp.take_along_axis(table, (jnp.arange(top)[None, :] + turn) % top, axis=1)


def load_shares(amount, total, most, lean, full):
    weights = [(1 << 20) // math.isqrt(grade ** lean) + 1 for grade in range(1, amount + 1)]
    largest = most if full else min(most, max(-(-total // amount), total * weights[0] // sum(weights)))
    least = 1 if total - largest >= amount - 1 else 0
    counts, spare = [largest] + [least] * (amount - 1), total - largest - least * (amount - 1)
    while spare > 0:
        free = [i for i in range(1, amount) if counts[i] < largest] or [i for i in range(1, amount) if counts[i] < most]
        pool, left = sum([weights[i] for i in free]), spare
        for i in free:
            extra = min(most - counts[i], max(1, left * weights[i] // pool), spare)
            counts[i] = counts[i] + extra
            spare = spare - extra
    return np.array(counts)


def centred(own_key, extent, spread, most, split=(), held_as=jnp.bfloat16):
    entries = spread * jax.random.normal(own_key, extent, jnp.float32)
    if split:
        entries = entries * steps_of(own_key, extent, split, -0.22, 0.18)
    return jnp.clip(entries, -most, most).astype(held_as)


def setup_inputs(seed: int = 0) -> dict:
    splits = jax.random.split(jax.random.key(seed), 8)
    tokens = centred(splits[0], (TOKENS, D), 1.0, 6.0, ((0, 64),))
    cotangent = centred(splits[1], (TOKENS, D), 1.0, 6.0, ((0, 64),))
    expert_ids_keys = jax.random.split(jax.random.fold_in(splits[2], 1), TOKENS // TOK_DEV)
    expert_ids_turns = jax.random.permutation(jax.random.fold_in(splits[2], 3), TOKENS // TOK_DEV)
    expert_ids = jax.vmap(lambda own, number: routed_block(jax.random.fold_in(splits[2], 2), own, number, TOK_DEV, EXPERTS, TOP, CAP, 1))(expert_ids_keys, expert_ids_turns).reshape((TOKENS, TOP))
    gate_probs = jnp.clip(jnp.exp(math.log(0.5) - 2.306499 * jax.random.uniform(splits[3], (TOKENS, TOP), jnp.float32) ** steps_of(splits[3], (TOKENS, TOP), ((0, 64),), -0.2, 0.2)), 0.049804688, 0.5).astype(jnp.bfloat16)
    w_gate = centred(splits[4], (EXPERTS, D, FF), D ** -0.5, 0.125, ((0, 64), (2, 8)))
    w_up = centred(splits[5], (EXPERTS, D, FF), D ** -0.5, 0.125, ((0, 64), (2, 8)))
    w_down = centred(splits[6], (EXPERTS, FF, D), FF ** -0.5, 0.1875, ((0, 64), (1, 8)))
    return dict(tokens=tokens, cotangent=cotangent, expert_ids=expert_ids, gate_probs=gate_probs, w_gate=w_gate, w_up=w_up, w_down=w_down)


def reference(tokens, cotangent, expert_ids, gate_probs, w_gate, w_up, w_down):
    routes = TOKENS * TOP
    width = N_EXPERT * CAP
    block = FF // N_TENSOR
    flat_e = expert_ids.reshape(-1).astype(jnp.int32)
    onehot = (flat_e[:, None] == jnp.arange(EXPERTS, dtype=jnp.int32)[None, :]).astype(jnp.int32)
    rank = jnp.sum(jnp.cumsum(onehot, axis=0) * onehot, axis=1) - 1
    table = jnp.full((EXPERTS * width,), routes, jnp.int32)
    table = table.at[(flat_e * width + rank).astype(jnp.int32)].set(jnp.arange(routes, dtype=jnp.int32))
    table = table.reshape(EXPERTS, width)
    flat_p = gate_probs.reshape(-1)

    def one_expert(total, inputs):
        entry, wgate, wup, wdown = inputs
        live = entry < routes
        safe = jnp.minimum(entry, routes - 1)
        owner = (safe // TOP).astype(jnp.int32)
        rows_x = jnp.where(live[:, None], tokens[owner], jnp.zeros((), tokens.dtype))
        rows_c = jnp.where(live[:, None], cotangent[owner], jnp.zeros((), cotangent.dtype))
        prob = jnp.where(live, flat_p[safe].astype(jnp.float32), jnp.float32(0.0))[:, None]
        gate = jnp.dot(rows_x, wgate, preferred_element_type=jnp.float32)
        upper = jnp.dot(rows_x, wup, preferred_element_type=jnp.float32)
        sig = jax.nn.sigmoid(gate)
        act = gate * sig
        dhid = prob * jnp.dot(rows_c, wdown.T, preferred_element_type=jnp.float32)
        scaled = (prob * act * upper).astype(jnp.bfloat16)
        dgate = (dhid * upper * sig * (1.0 + gate * (1.0 - sig))).astype(jnp.bfloat16)
        dup = (dhid * act).astype(jnp.bfloat16)
        gdown = jnp.dot(scaled.T, rows_c, preferred_element_type=jnp.float32).astype(jnp.bfloat16)
        ggate = jnp.dot(rows_x.T, dgate, preferred_element_type=jnp.float32).astype(jnp.bfloat16)
        gup = jnp.dot(rows_x.T, dup, preferred_element_type=jnp.float32).astype(jnp.bfloat16)
        dg3 = dgate.astype(jnp.float32).reshape(width, N_TENSOR, block)
        du3 = dup.astype(jnp.float32).reshape(width, N_TENSOR, block)
        wg3 = wgate.astype(jnp.float32).reshape(D, N_TENSOR, block)
        wu3 = wup.astype(jnp.float32).reshape(D, N_TENSOR, block)
        piece = jnp.einsum("rjf,djf->rjd", dg3, wg3) + jnp.einsum("rjf,djf->rjd", du3, wu3)
        piece = lax.optimization_barrier(piece.astype(jnp.bfloat16))
        summed = jnp.sum(piece.astype(jnp.float32), axis=1)
        summed = jnp.where(live[:, None], summed, jnp.float32(0.0))
        total = total.at[owner].add(summed)
        return total, (ggate, gup, gdown)

    start = jnp.zeros((TOKENS, D), jnp.float32)
    total, grads = lax.scan(one_expert, start, (table, w_gate, w_up, w_down))
    return total.astype(jnp.bfloat16), grads[0], grads[1], grads[2]
```

```python
import functools

import jax
import jax.numpy as jnp
import ml_dtypes
import numpy as np
from jax import lax
from jax.experimental import pallas as pl
from jax.experimental.pallas import tpu as pltpu
from jax.sharding import PartitionSpec as P

MESH = pl.DeviceIdType.MESH
BF = jnp.bfloat16
F32 = jnp.float32
CAP = 20
SIDE = 4
LANES = 128
PART = 256
OUT = 4 * CAP
BACK = 48


def dot(a, b):
    return jnp.dot(a, b, preferred_element_type=F32)


def dot_t(a, b):
    return lax.dot_general(a, b, (((1,), (1,)), ((), ())), preferred_element_type=F32)


def t_dot(a, b):
    return lax.dot_general(a, b, (((0,), (0,)), ((), ())), preferred_element_type=F32)


def kernel(
    ne, nt, side, gp,
    ids_ref, idst_ref, probst_ref, tok_ref, cot_ref, wg_ref, wu_ref, wd_ref,
    perm_ref, back_ref, expand_ref, phase_ref,
    gi_ref, gg_ref, gu_ref, gd_ref,
    key_ref, pr_ref, rhs_ref, sel_ref, send_ref, recv_ref, g_ref, w_ref, d_ref, sc_ref,
    rs_send, rs_recv, ret_send, ret_recv, lo_ref, hi_ref,
    a2a_s, a2a_r, ag_s, ag_r, rs_s, rs_r, ret_s, ret_r,
):
    wide = 2 * side
    ny = ne // wide
    half = nt // 2
    rows = wide * CAP
    tokens = tok_ref.shape[0]
    ei, ti = lax.axis_index("expert"), lax.axis_index("tensor")
    yy, xx, core = ei // wide, lax.rem(ei // 2, side), lax.rem(ei, 2)
    right, left = lax.rem(ti + 1, nt), lax.rem(ti + nt - 1, nt)
    opp = lax.rem(ti + half, nt)

    def away(c):
        h, odd = (c + 1) // 2, lax.rem(c, 2)
        return odd * h + (1 - odd) * (ny - h)

    def row_to(c):
        return lax.rem(yy + 2 * ny - away(c), ny)

    def peer_to(c, s):
        dx, dc = s // 2, s % 2
        return row_to(c) * wide + lax.rem(xx + side - dx, side) * 2 + lax.rem(core + dc, 2)

    def peer_from(c, s):
        dx, dc = s // 2, s % 2
        return (
            lax.rem(yy + away(c), ny) * wide
            + lax.rem(xx + dx, side) * 2
            + lax.rem(core + dc, 2)
        )

    def others(act):
        for s in range(1, wide):
            act(0, s)

        @pl.loop(1, ny)
        def _(c):
            for s in range(wide):
                act(c, s)

    bar = pltpu.get_barrier_semaphore()
    others(
        lambda c, s: pl.semaphore_signal(
            bar, inc=1, device_id=(peer_to(c, s), ti), device_id_type=MESH
        )
    )
    for z in (right, left):
        pl.semaphore_signal(bar, inc=1, device_id=(ei, z), device_id_type=MESH)

    hits = jnp.zeros((ne, tokens), F32)
    prob = jnp.zeros((ne, tokens), F32)
    experts = lax.broadcasted_iota(jnp.int32, (ne, tokens), 0)
    for k in range(idst_ref.shape[0]):
        hit = idst_ref[k : k + 1, :] == experts
        hits = jnp.where(hit, 1.0, hits)
        prob = jnp.where(hit, probst_ref[k : k + 1, :], prob)
    r0 = lax.broadcasted_iota(jnp.int32, (tokens, tokens), 0)
    r1 = lax.broadcasted_iota(jnp.int32, (tokens, tokens), 1)
    before = jnp.where(r0 < r1, 1.0, 0.0).astype(BF)
    key_ref[...] = jnp.where(hits > 0.0, dot(hits.astype(BF), before), -1000.0)
    pr_ref[...] = prob

    for j in range(2):
        for m, start in enumerate((ti, opp)):
            at = pl.multiple_of(start * PART + j * LANES, LANES)
            cols = slice(m * LANES, (m + 1) * LANES)
            rhs_ref[j * tokens : (j + 1) * tokens, cols] = tok_ref[:, pl.ds(at, LANES)]
            rhs_ref[(2 + j) * tokens : (3 + j) * tokens, cols] = cot_ref[:, pl.ds(at, LANES)]

    def send_copy(c, s):
        to = peer_to(c, s)
        return pltpu.make_async_remote_copy(
            src_ref=send_ref.at[pl.ds(pl.multiple_of(to * OUT, OUT), OUT)],
            dst_ref=recv_ref.at[pl.ds(pl.multiple_of((c * wide + s) * OUT, OUT), OUT)],
            send_sem=a2a_s,
            recv_sem=a2a_r.at[c],
            device_id=(to, ti),
            device_id_type=MESH,
        )

    def pack(c):
        first = row_to(c) * wide
        keys = key_ref[pl.ds(pl.multiple_of(first, wide), wide), :]
        probs = pr_ref[pl.ds(pl.multiple_of(first, wide), wide), :]
        place = lax.broadcasted_iota(jnp.int32, (OUT, tokens), 0).astype(F32)
        for i in range(wide):
            key = jnp.broadcast_to(keys[i : i + 1, :], (OUT, tokens))
            share = jnp.broadcast_to(probs[i : i + 1, :], (OUT, tokens))
            for j in range(4):
                value = 1.0 if j < 2 else share
                sel_ref[i * OUT : (i + 1) * OUT, j * tokens : (j + 1) * tokens] = jnp.where(
                    place - float(CAP * j) == key, value, 0.0
                ).astype(BF)
        at = pl.ds(pl.multiple_of(first * OUT, OUT), wide * OUT)
        send_ref[at, :] = dot(sel_ref[...], rhs_ref[...]).astype(BF)

    pack(0)
    own = pltpu.make_async_copy(
        send_ref.at[pl.ds(pl.multiple_of(ei * OUT, OUT), OUT)],
        recv_ref.at[pl.ds(0, OUT)],
        a2a_r.at[0],
    )
    own.start()
    pl.semaphore_wait(bar, ne + 1)
    for s in range(1, wide):
        send_copy(0, s).start()

    @pl.loop(1, ny)
    def _(c):
        pack(c)
        for s in range(wide):
            send_copy(c, s).start()

    w_ref[:, :LANES] = wg_ref[...]
    w_ref[:, LANES:] = wu_ref[...]

    def block(c):
        return pl.ds(pl.multiple_of(c * rows, rows), rows)

    def ag_copy(c, s, way):
        unit = lax.rem(ti + nt - s, nt) if way == 0 else lax.rem(ti + s, nt)
        ref = g_ref.at[unit, block(c)]
        return pltpu.make_async_remote_copy(
            src_ref=ref,
            dst_ref=ref,
            send_sem=ag_s.at[way, s],
            recv_sem=ag_r.at[way, s, c],
            device_id=(ei, right if way == 0 else left),
            device_id_type=MESH,
        )

    def arrive(c):
        got = recv_ref.at[pl.ds(pl.multiple_of(c * wide * OUT, OUT), wide * OUT)]
        pltpu.make_async_copy(got, got, a2a_r.at[c]).wait()
        for g in range(wide // gp):
            at = pl.multiple_of((c * wide + g * gp) * OUT, OUT)
            out = dot(perm_ref[...], recv_ref[pl.ds(at, gp * OUT), :]).astype(BF)
            to = pl.ds(pl.multiple_of(c * rows + g * gp * CAP, gp * CAP), gp * CAP)
            for j in range(4):
                piece = out[j * gp * CAP : (j + 1) * gp * CAP, :]
                g_ref[ti, to, j * LANES : (j + 1) * LANES] = piece[:, :LANES]
                g_ref[opp, to, j * LANES : (j + 1) * LANES] = piece[:, LANES:]
        for way in range(2):
            ag_copy(c, 0, way).start()

    def ag_wait(c, s):
        for way in range(2):
            unit = lax.rem(ti + nt - s - 1, nt) if way == 0 else lax.rem(ti + s + 1, nt)
            ref = g_ref.at[unit, block(c)]
            pltpu.make_async_copy(ref, ref, ag_r.at[way, s, c]).wait()

    def forward(s, c):
        ag_wait(c, s - 1)
        for way in range(2):
            ag_copy(c, s, way).start()

    def piece_of(c, target):
        at = pl.ds(pl.multiple_of(target * PART, PART), PART)
        return dot_t(d_ref[block(c), :], w_ref[at, :])

    def rs_rows(c, k, way):
        if k > 0:
            return block(c)
        return pl.ds(pl.multiple_of(c * rows + way * (rows // 2), rows // 2), rows // 2)

    def rs_copy(c, k, way):
        at = rs_rows(c, k, way)
        return pltpu.make_async_remote_copy(
            src_ref=rs_send.at[0 if k == 0 else way, k, at],
            dst_ref=rs_recv.at[way, k, at],
            send_sem=rs_s.at[way, k],
            recv_sem=rs_r.at[way, k, c],
            device_id=(ei, right if way == 0 else left),
            device_id_type=MESH,
        )

    def rs_wait(c, k, way):
        ref = rs_recv.at[way, k, rs_rows(c, k, way)]
        pltpu.make_async_copy(ref, ref, rs_r.at[way, k, c]).wait()

    def middle(c):
        ag_wait(c, half - 2)
        at = block(c)
        both = jnp.zeros((rows, 2 * LANES), F32)
        dhid = jnp.zeros((rows, LANES), F32)
        for u in range(nt):
            cols = slice(u * PART, (u + 1) * PART)
            both = both + dot(g_ref[u, at, :PART], w_ref[cols, :])
            dhid = dhid + dot_t(g_ref[u, at, PART:], wd_ref[:, cols])
        gate, upper = both[:, :LANES], both[:, LANES:]
        sig = 1.0 / (1.0 + jnp.exp(-gate))
        act = gate * sig
        sc_ref[at, :] = (act * upper).astype(BF)
        d_ref[at, :LANES] = (dhid * upper * sig * (1.0 + gate * (1.0 - sig))).astype(BF)
        d_ref[at, LANES:] = (dhid * act).astype(BF)
        rs_send[0, 0, at, :] = piece_of(c, opp).astype(BF)
        for way in range(2):
            rs_copy(c, 0, way).start()

    def add(k, c):
        for way in range(2):
            hop = half - k
            target = lax.rem(ti + hop, nt) if way == 0 else lax.rem(ti + nt - hop, nt)
            piece = piece_of(c, target)
            rs_wait(c, k - 1, way)
            if k > 1:
                got = rs_recv[way, k - 1, block(c), :].astype(F32)
                rs_send[way, k, block(c), :] = (piece + got).astype(BF)
            else:
                for part in range(2):
                    at = rs_rows(c, 0, part)
                    here = piece[part * (rows // 2) : (part + 1) * (rows // 2), :]
                    if part == way:
                        here = here + rs_recv[way, 0, at, :].astype(F32)
                    rs_send[way, k, at, :] = here.astype(BF)
            rs_copy(c, k, way).start()

    def back_copy(c, s):
        return pltpu.make_async_remote_copy(
            src_ref=ret_send.at[pl.ds(pl.multiple_of((c * wide + s) * BACK, BACK), BACK)],
            dst_ref=ret_recv.at[pl.ds(pl.multiple_of(ei * BACK, BACK), BACK)],
            send_sem=ret_s,
            recv_sem=ret_r.at[c],
            device_id=(peer_from(c, s), ti),
            device_id_type=MESH,
        )

    def finish(c):
        piece = piece_of(c, ti)
        for way in range(2):
            rs_wait(c, half - 1, way)
            piece = piece + rs_recv[way, half - 1, block(c), :].astype(F32)
        whole = piece.astype(BF)
        at = pl.ds(pl.multiple_of(c * wide * BACK, BACK), wide * BACK)
        ret_send[at, :] = (
            dot(back_ref[0], whole[:, :LANES]) + dot(back_ref[1], whole[:, LANES:])
        ).astype(BF)

        @pl.when(c == 0)
        def _():
            pltpu.make_async_copy(
                ret_send.at[pl.ds(0, BACK)],
                ret_recv.at[pl.ds(pl.multiple_of(ei * BACK, BACK), BACK)],
                ret_r.at[c],
            ).start()

        @pl.when(c != 0)
        def _():
            back_copy(c, 0).start()

        for s in range(1, wide):
            back_copy(c, s).start()

    def weight_grads(u):
        at = pl.ds(pl.multiple_of(u * PART, PART), PART)
        both = t_dot(g_ref[u, :, :PART], d_ref[...]).astype(BF)
        gg_ref[at, :] = both[:, :LANES]
        gu_ref[at, :] = both[:, LANES:]
        gd_ref[:, at] = t_dot(sc_ref[...], g_ref[u, :, PART:]).astype(BF)

    stages = [arrive]
    stages += [functools.partial(forward, s) for s in range(1, half - 1)]
    stages += [middle]
    stages += [functools.partial(add, k) for k in range(1, half)]
    stages += [finish]

    hits_n = jnp.zeros((tokens, ne), F32)
    experts_n = lax.broadcasted_iota(jnp.int32, (tokens, ne), 1)
    for k in range(ids_ref.shape[1]):
        hits_n = jnp.where(ids_ref[:, k : k + 1] == experts_n, 1.0, hits_n)
    after = jnp.where(r1 < r0, 1.0, 0.0).astype(BF)
    key_n = jnp.where(hits_n > 0.0, dot(after, hits_n.astype(BF)), 200.0).astype(BF)
    tile = min(ne * BACK, 512)
    for n in range(0, ne * BACK, tile):
        want = dot(key_n, expand_ref[:, n : n + tile])
        phase = phase_ref[:, n : n + tile]
        lo_ref[:, n : n + tile] = jnp.where(want == phase, 1.0, 0.0).astype(BF)
        hi_ref[:, n : n + tile] = jnp.where(want + float(CAP) == phase, 1.0, 0.0).astype(BF)

    last = ny + half - 1
    each = nt // half

    @pl.loop(0, ny + len(stages) - 1)
    def _(turn):
        for i, stage in enumerate(stages):
            c = turn - i
            pl.when(jnp.logical_and(c >= 0, c < ny))(functools.partial(stage, c))

        @pl.when(turn >= last)
        def _():
            for i in range(each):
                weight_grads((turn - last) * each + i)

    @pl.loop(0, ny)
    def _(c):
        got = ret_recv.at[pl.ds(pl.multiple_of(c * wide * BACK, BACK), wide * BACK)]
        pltpu.make_async_copy(got, got, ret_r.at[c]).wait()

    gi_ref[:, :LANES] = dot(lo_ref[...], ret_recv[...]).astype(BF)
    gi_ref[:, LANES:] = dot(hi_ref[...], ret_recv[...]).astype(BF)

    sent = send_ref.at[pl.ds(0, (ne - 1) * OUT)]
    pltpu.make_async_copy(sent, sent, a2a_s).wait()
    sent = ret_send.at[pl.ds(0, (ne - 1) * BACK)]
    pltpu.make_async_copy(sent, sent, ret_s).wait()
    for way in range(2):
        for s in range(half - 1):
            pltpu.make_async_copy(g_ref.at[0], g_ref.at[0], ag_s.at[way, s]).wait()
        for k in range(half):
            sent = rs_send.at[0, 0]
            if k == 0:
                sent = rs_send.at[0, 0, pl.ds(0, ny * (rows // 2))]
            pltpu.make_async_copy(sent, sent, rs_s.at[way, k]).wait()


def tables(ne, side):
    wide = 2 * side
    gp = min(4, wide)
    perm = np.zeros((gp * OUT, gp * OUT), np.float32)
    for j in range(4):
        for s in range(gp):
            for r in range(CAP):
                perm[j * gp * CAP + s * CAP + r, s * OUT + j * CAP + r] = 1.0
    back = np.zeros((2, wide * BACK, wide * CAP), np.float32)
    for s in range(wide):
        for r in range(CAP):
            for m in range(2):
                back[m, s * BACK + m * CAP + r, s * CAP + r] = 1.0
    expand = np.kron(np.eye(ne, dtype=np.float32), np.ones((1, BACK), np.float32))
    phase = np.tile(np.arange(BACK, dtype=np.float32), ne)[None, :]
    half = ml_dtypes.bfloat16
    return gp, perm.astype(half), back.astype(half), expand.astype(half), phase


def solution(mesh):
    ne, nt = mesh.shape["expert"], mesh.shape["tensor"]
    side = SIDE
    wide = 2 * side
    ny, half = ne // wide, nt // 2
    rows = ne * CAP
    gp, perm, back, expand, phase = tables(ne, side)

    def step(tokens, cotangent, expert_ids, gate_probs, w_gate, w_up, w_down):
        owned, width = tokens.shape
        vmem = pl.BlockSpec(memory_space=pltpu.VMEM)
        dma = pltpu.SemaphoreType.DMA
        gi, gg, gu, gd = pl.pallas_call(
            functools.partial(kernel, ne, nt, side, gp),
            out_shape=(
                jax.ShapeDtypeStruct((owned, PART), BF),
                jax.ShapeDtypeStruct((width, LANES), BF),
                jax.ShapeDtypeStruct((width, LANES), BF),
                jax.ShapeDtypeStruct((LANES, width), BF),
            ),
            in_specs=[vmem] * 12,
            out_specs=(vmem,) * 4,
            scratch_shapes=[
                pltpu.VMEM((ne, owned), F32),
                pltpu.VMEM((ne, owned), F32),
                pltpu.VMEM((4 * owned, 2 * LANES), BF),
                pltpu.VMEM((wide * OUT, 4 * owned), BF),
                pltpu.VMEM((ne * OUT, 2 * LANES), BF),
                pltpu.VMEM((ne * OUT, 2 * LANES), BF),
                pltpu.VMEM((nt, rows, 2 * PART), BF),
                pltpu.VMEM((width, 2 * LANES), BF),
                pltpu.VMEM((rows, 2 * LANES), BF),
                pltpu.VMEM((rows, LANES), BF),
                pltpu.VMEM((2, half, rows, PART), BF),
                pltpu.VMEM((2, half, rows, PART), BF),
                pltpu.VMEM((ne * BACK, LANES), BF),
                pltpu.VMEM((ne * BACK, LANES), BF),
                pltpu.VMEM((owned, ne * BACK), BF),
                pltpu.VMEM((owned, ne * BACK), BF),
                dma,
                dma((ny,)),
                dma((2, half - 1)),
                dma((2, half - 1, ny)),
                dma((2, half)),
                dma((2, half, ny)),
                dma,
                dma((ny,)),
            ],
            compiler_params=pltpu.CompilerParams(
                collective_id=0, has_side_effects=True, vmem_limit_bytes=56 * 1024 * 1024
            ),
        )(
            expert_ids,
            expert_ids.T,
            gate_probs.T.astype(F32),
            tokens,
            cotangent,
            w_gate[0],
            w_up[0],
            w_down[0],
            jnp.asarray(perm),
            jnp.asarray(back),
            jnp.asarray(expand),
            jnp.asarray(phase),
        )
        return gi, gg[None], gu[None], gd[None]

    return jax.shard_map(
        step,
        mesh=mesh,
        in_specs=(
            P("expert", None),
            P("expert", None),
            P("expert", None),
            P("expert", None),
            P("expert", None, "tensor"),
            P("expert", None, "tensor"),
            P("expert", "tensor", None),
        ),
        out_specs=(
            P("expert", "tensor"),
            P("expert", None, "tensor"),
            P("expert", None, "tensor"),
            P("expert", "tensor", None),
        ),
        check_vma=False,
    )
```

```python
import functools

import jax
import jax.numpy as jnp
import ml_dtypes
import numpy as np
from jax import lax
from jax.experimental import pallas as pl
from jax.experimental.pallas import tpu as pltpu
from jax.sharding import PartitionSpec as P

MESH = pl.DeviceIdType.MESH
BF = jnp.bfloat16
F32 = jnp.float32
CAP = 20
SIDE = 4
LANES = 128
PART = 256
OUT = 4 * CAP
BACK = 48
AHEAD = 1
LAG = 1


def ring_chunks(ny):
    return ny - 2 if ny > 4 else ny - 1


def dot(a, b):
    return jnp.dot(a, b, preferred_element_type=F32)


def dot_t(a, b):
    return lax.dot_general(a, b, (((1,), (1,)), ((), ())), preferred_element_type=F32)


def t_dot(a, b):
    return lax.dot_general(a, b, (((0,), (0,)), ((), ())), preferred_element_type=F32)


def kernel(
    ne, nt, side, gp,
    idst_ref, probst_ref, tok_ref, cot_ref, wg_ref, wu_ref, wd_ref,
    perm_ref, back_ref, expand_ref, phase_ref,
    gi_ref, gg_ref, gu_ref, gd_ref,
    key_ref, pr_ref, rhs_ref, all_ref, sel_ref, send_ref, recv_ref, nsend_ref, nrecv_ref, g_ref, w_ref, d_ref, sc_ref,
    rs_send, rs_recv, ret_send, ret_recv, lo_ref, hi_ref,
    a2a_s, near_s, a2a_r, ag_s, ag_r, rs_s, rs_r, ret_s, ret_r,
):
    wide = 2 * side
    ny = ne // wide
    half = nt // 2
    rows = wide * CAP
    ring = ring_chunks(ny)
    tokens = tok_ref.shape[0]
    ei, ti = lax.axis_index("expert"), lax.axis_index("tensor")
    yy, xx, core = ei // wide, lax.rem(ei // 2, side), lax.rem(ei, 2)
    right, left = lax.rem(ti + 1, nt), lax.rem(ti + nt - 1, nt)
    opp = lax.rem(ti + half, nt)

    def away(c):
        c = (lax.rem(c + 1, ny - 1) + 1) * jnp.minimum(c, 1)
        h, odd = (c + 1) // 2, lax.rem(c, 2)
        return odd * h + (1 - odd) * (ny - h)

    def row_to(c):
        return lax.rem(yy + 2 * ny - away(c), ny)

    def peer_to(c, s):
        dx, dc = s // 2, lax.rem(s, 2)
        return row_to(c) * wide + lax.rem(xx + side - dx, side) * 2 + lax.rem(core + dc, 2)

    def peer_from(c, s):
        dx, dc = s // 2, lax.rem(s, 2)
        return (
            lax.rem(yy + away(c), ny) * wide
            + lax.rem(xx + dx, side) * 2
            + lax.rem(core + dc, 2)
        )

    def turned(i):
        return lax.rem(i + core * (wide // 2), wide)

    def others(act):
        for s in range(1, wide):
            act(0, s)

        @pl.loop(1, ny)
        def _(c):
            for s in range(wide):
                act(c, s)

    bar = pltpu.get_barrier_semaphore()
    others(
        lambda c, s: pl.semaphore_signal(
            bar, inc=1, device_id=(peer_to(c, s), ti), device_id_type=MESH
        )
    )
    for z in (right, left):
        pl.semaphore_signal(bar, inc=1, device_id=(ei, z), device_id_type=MESH)

    hits = jnp.zeros((ne, tokens), F32)
    prob = jnp.zeros((ne, tokens), F32)
    experts = lax.broadcasted_iota(jnp.int32, (ne, tokens), 0)
    given = probst_ref[...].astype(F32)
    for k in range(idst_ref.shape[0]):
        hit = idst_ref[k : k + 1, :] == experts
        hits = jnp.where(hit, 1.0, hits)
        prob = jnp.where(hit, given[k : k + 1, :], prob)
    r0 = lax.broadcasted_iota(jnp.int32, (tokens, tokens), 0)
    r1 = lax.broadcasted_iota(jnp.int32, (tokens, tokens), 1)
    before = jnp.where(r0 < r1, 1.0, 0.0).astype(BF)
    key_ref[...] = jnp.where(hits > 0.0, dot(hits.astype(BF), before), -1000.0)
    pr_ref[...] = prob

    for j in range(2):
        for u in range(nt):
            cols = slice(u * LANES, (u + 1) * LANES)
            at = slice(u * PART + j * LANES, u * PART + (j + 1) * LANES)
            all_ref[j * tokens : (j + 1) * tokens, cols] = tok_ref[:, at]
            all_ref[(2 + j) * tokens : (3 + j) * tokens, cols] = cot_ref[:, at]
    for m, start in enumerate((ti, opp)):
        at = pl.ds(pl.multiple_of(start * LANES, LANES), LANES)
        rhs_ref[:, m * LANES : (m + 1) * LANES] = all_ref[:, at]

    def send_copy(c, s, near):
        to = peer_to(c, s)
        src, dst, first = (nsend_ref, nrecv_ref, ring) if near else (send_ref, recv_ref, 0)
        row = (c - first) * wide
        return pltpu.make_async_remote_copy(
            src_ref=src.at[
                pl.ds(pl.multiple_of((row + to - row_to(c) * wide) * OUT, OUT), OUT)
            ],
            dst_ref=dst.at[pl.ds(pl.multiple_of((row + s) * OUT, OUT), OUT)],
            send_sem=near_s if near else a2a_s,
            recv_sem=a2a_r.at[c],
            device_id=(to, ti),
            device_id_type=MESH,
        )

    def select(c):
        first = row_to(c) * wide
        keys = key_ref[pl.ds(pl.multiple_of(first, wide), wide), :]
        probs = pr_ref[pl.ds(pl.multiple_of(first, wide), wide), :]
        place = lax.broadcasted_iota(jnp.int32, (OUT, tokens), 0).astype(F32)
        for i in range(wide):
            key = jnp.broadcast_to(keys[i : i + 1, :], (OUT, tokens))
            share = jnp.broadcast_to(probs[i : i + 1, :], (OUT, tokens))
            for j in range(4):
                value = 1.0 if j < 2 else share
                sel_ref[i * OUT : (i + 1) * OUT, j * tokens : (j + 1) * tokens] = jnp.where(
                    place - float(CAP * j) == key, value, 0.0
                ).astype(BF)

    def far_rows(c):
        return pl.ds(pl.multiple_of(c * wide * OUT, OUT), wide * OUT)

    def pack(c):
        select(c)
        if isinstance(c, int) and c >= ring:
            nsend_ref[far_rows(c - ring), :] = dot(sel_ref[...], all_ref[...]).astype(BF)
        else:
            send_ref[far_rows(c), :] = dot(sel_ref[...], rhs_ref[...]).astype(BF)

    def send(chunks):
        for c in chunks:
            pack(c)
        for i in range(wide):
            for c in chunks:
                send_copy(c, turned(i), c >= ring).start()

    groups = [range(c, min(c + 2, ring)) for c in range(1, ring, 2)] + [range(ring, ny)]

    pack(0)
    mine = ei - yy * wide
    own = pltpu.make_async_copy(
        send_ref.at[pl.ds(pl.multiple_of(mine * OUT, OUT), OUT)],
        recv_ref.at[pl.ds(0, OUT)],
        a2a_r.at[0],
    )
    own.start()
    pl.semaphore_wait(bar, ne + 1)
    for s in range(1, wide):
        send_copy(0, s, False).start()

    for group in groups[:AHEAD]:
        send(group)

    def prepare():
        w_ref[:, :LANES] = wg_ref[...]
        w_ref[:, LANES:] = wu_ref[...]

    def block(c):
        return pl.ds(pl.multiple_of(c * rows, rows), rows)

    def ag_copy(c, s, way):
        unit = lax.rem(ti + nt - s, nt) if way == 0 else lax.rem(ti + s, nt)
        ref = g_ref.at[unit, block(c)]
        return pltpu.make_async_remote_copy(
            src_ref=ref,
            dst_ref=ref,
            send_sem=ag_s.at[way, s],
            recv_sem=ag_r.at[way, s, c],
            device_id=(ei, right if way == 0 else left),
            device_id_type=MESH,
        )

    def arrive(c):
        got = recv_ref.at[pl.ds(pl.multiple_of(c * wide * OUT, OUT), wide * OUT)]
        pltpu.make_async_copy(got, got, a2a_r.at[c]).wait()
        for g in range(wide // gp):
            at = pl.multiple_of((c * wide + g * gp) * OUT, OUT)
            out = dot(perm_ref[...], recv_ref[pl.ds(at, gp * OUT), :]).astype(BF)
            to = pl.ds(pl.multiple_of(c * rows + g * gp * CAP, gp * CAP), gp * CAP)
            for j in range(4):
                piece = out[j * gp * CAP : (j + 1) * gp * CAP, :]
                g_ref[ti, to, j * LANES : (j + 1) * LANES] = piece[:, :LANES]
                g_ref[opp, to, j * LANES : (j + 1) * LANES] = piece[:, LANES:]
        for way in range(2):
            ag_copy(c, 0, way).start()

    def direct(c):
        got = nrecv_ref.at[far_rows(c - ring)]
        pltpu.make_async_copy(got, got, a2a_r.at[c]).wait()
        for g in range(wide // gp):
            at = pl.multiple_of(((c - ring) * wide + g * gp) * OUT, OUT)
            to = pl.ds(pl.multiple_of(c * rows + g * gp * CAP, gp * CAP), gp * CAP)
            for u in range(0, nt, 2):
                cols = slice(u * LANES, (u + 2) * LANES)
                out = dot(perm_ref[...], nrecv_ref[pl.ds(at, gp * OUT), cols]).astype(BF)
                for j in range(4):
                    piece = out[j * gp * CAP : (j + 1) * gp * CAP, :]
                    g_ref[u, to, j * LANES : (j + 1) * LANES] = piece[:, :LANES]
                    g_ref[u + 1, to, j * LANES : (j + 1) * LANES] = piece[:, LANES:]
        hidden(c)

    def ag_wait(c, s):
        for way in range(2):
            unit = lax.rem(ti + nt - s - 1, nt) if way == 0 else lax.rem(ti + s + 1, nt)
            ref = g_ref.at[unit, block(c)]
            pltpu.make_async_copy(ref, ref, ag_r.at[way, s, c]).wait()

    def forward(s, c):
        ag_wait(c, s - 1)
        for way in range(2):
            ag_copy(c, s, way).start()

    def piece_of(c, target):
        at = pl.ds(pl.multiple_of(target * PART, PART), PART)
        return dot_t(d_ref[block(c), :], w_ref[at, :])

    def rs_rows(c, k, way):
        if k > 0:
            return block(c)
        return pl.ds(pl.multiple_of(c * rows + way * (rows // 2), rows // 2), rows // 2)

    def rs_copy(c, k, way):
        at = rs_rows(c, k, way)
        return pltpu.make_async_remote_copy(
            src_ref=rs_send.at[0 if k == 0 else way, k, at],
            dst_ref=rs_recv.at[way, k, at],
            send_sem=rs_s.at[way, k],
            recv_sem=rs_r.at[way, k, c],
            device_id=(ei, right if way == 0 else left),
            device_id_type=MESH,
        )

    def rs_wait(c, k, way):
        ref = rs_recv.at[way, k, rs_rows(c, k, way)]
        pltpu.make_async_copy(ref, ref, rs_r.at[way, k, c]).wait()

    def middle(c):
        ag_wait(c, half - 2)
        hidden(c)

    def hidden(c):
        at = block(c)
        both = jnp.zeros((rows, 2 * LANES), F32)
        dhid = jnp.zeros((rows, LANES), F32)
        for u in range(nt):
            cols = slice(u * PART, (u + 1) * PART)
            both = both + dot(g_ref[u, at, :PART], w_ref[cols, :])
            dhid = dhid + dot_t(g_ref[u, at, PART:], wd_ref[:, cols])
        gate, upper = both[:, :LANES], both[:, LANES:]
        sig = 1.0 / (1.0 + jnp.exp(-gate))
        act = gate * sig
        sc_ref[at, :] = (act * upper).astype(BF)
        d_ref[at, :LANES] = (dhid * upper * sig * (1.0 + gate * (1.0 - sig))).astype(BF)
        d_ref[at, LANES:] = (dhid * act).astype(BF)
        rs_send[0, 0, at, :] = piece_of(c, opp).astype(BF)
        for way in range(2):
            rs_copy(c, 0, way).start()

    def add(k, c):
        for way in range(2):
            hop = half - k
            target = lax.rem(ti + hop, nt) if way == 0 else lax.rem(ti + nt - hop, nt)
            piece = piece_of(c, target)
            rs_wait(c, k - 1, way)
            if k > 1:
                got = rs_recv[way, k - 1, block(c), :].astype(F32)
                rs_send[way, k, block(c), :] = (piece + got).astype(BF)
            else:
                for part in range(2):
                    at = rs_rows(c, 0, part)
                    here = piece[part * (rows // 2) : (part + 1) * (rows // 2), :]
                    if part == way:
                        here = here + rs_recv[way, 0, at, :].astype(F32)
                    rs_send[way, k, at, :] = here.astype(BF)
            rs_copy(c, k, way).start()

    def back_copy(c, s):
        return pltpu.make_async_remote_copy(
            src_ref=ret_send.at[pl.ds(pl.multiple_of((c * wide + s) * BACK, BACK), BACK)],
            dst_ref=ret_recv.at[pl.ds(pl.multiple_of(ei * BACK, BACK), BACK)],
            send_sem=ret_s,
            recv_sem=ret_r.at[c],
            device_id=(peer_from(c, s), ti),
            device_id_type=MESH,
        )

    def finish(c):
        piece = piece_of(c, ti)
        for way in range(2):
            rs_wait(c, half - 1, way)
            piece = piece + rs_recv[way, half - 1, block(c), :].astype(F32)
        whole = piece.astype(BF)
        at = pl.ds(pl.multiple_of(c * wide * BACK, BACK), wide * BACK)
        ret_send[at, :] = (
            dot(back_ref[0], whole[:, :LANES]) + dot(back_ref[1], whole[:, LANES:])
        ).astype(BF)

        @pl.when(c == 0)
        def _():
            pltpu.make_async_copy(
                ret_send.at[pl.ds(0, BACK)],
                ret_recv.at[pl.ds(pl.multiple_of(ei * BACK, BACK), BACK)],
                ret_r.at[c],
            ).start()
            for s in range(1, wide):
                back_copy(c, s).start()

        @pl.when(c != 0)
        def _():
            for i in range(wide):
                back_copy(c, turned(i)).start()

    def weight_grads(u):
        at = pl.ds(pl.multiple_of(u * PART, PART), PART)
        both = t_dot(g_ref[u, :, :PART], d_ref[...]).astype(BF)
        gg_ref[at, :] = both[:, :LANES]
        gu_ref[at, :] = both[:, LANES:]
        gd_ref[:, at] = t_dot(sc_ref[...], g_ref[u, :, PART:]).astype(BF)

    sums = [functools.partial(add, k) for k in range(1, half)] + [finish]
    stages = [arrive] + [functools.partial(forward, s) for s in range(1, half - 1)]
    stages += [middle] + sums

    def places():
        e0 = lax.broadcasted_iota(jnp.int32, (ne, ne), 0)
        e1 = lax.broadcasted_iota(jnp.int32, (ne, ne), 1)
        hits_n = t_dot(hits.astype(BF), jnp.where(e0 == e1, 1.0, 0.0).astype(BF))
        after = jnp.where(r1 < r0, 1.0, 0.0).astype(BF)
        key_n = jnp.where(hits_n > 0.0, dot(after, hits_n.astype(BF)), 200.0).astype(BF)
        tile = min(ne * BACK, 512)
        for n in range(0, ne * BACK, tile):
            want = dot(key_n, expand_ref[:, n : n + tile])
            phase = phase_ref[:, n : n + tile]
            lo_ref[:, n : n + tile] = jnp.where(want == phase, 1.0, 0.0).astype(BF)
            hi_ref[:, n : n + tile] = jnp.where(want + float(CAP) == phase, 1.0, 0.0).astype(BF)

    turns = max(ring - 1 + len(stages), ny - 1 + LAG + len(sums) + 1)
    last = max(ring + half - 1, ny + LAG)
    each = -(-nt // (turns - last))

    @pl.loop(0, turns)
    def _(turn):
        for i, group in enumerate(groups[AHEAD:]):
            pl.when(turn == i)(functools.partial(send, group))
        for i, stage in enumerate(stages):
            c = turn - i
            pl.when(jnp.logical_and(c >= 0, c < ring))(functools.partial(stage, c))
            if i == 0:
                pl.when(turn == 0)(prepare)
                pl.when(turn == 1)(places)
        for i, stage in enumerate([direct] + sums):
            c = turn - i - LAG
            pl.when(jnp.logical_and(c >= ring, c < ny))(functools.partial(stage, c))
        for i in range(each):
            u = (turn - last) * each + i
            pl.when(jnp.logical_and(turn >= last, u < nt))(functools.partial(weight_grads, u))

    low = jnp.zeros((tokens, LANES), F32)
    high = jnp.zeros((tokens, LANES), F32)
    for c in range(ny):
        at = pl.ds(pl.multiple_of(row_to(c) * wide * BACK, wide * BACK), wide * BACK)
        got = ret_recv.at[at]
        pltpu.make_async_copy(got, got, ret_r.at[c]).wait()
        low = low + dot(lo_ref[:, at], ret_recv[at, :])
        high = high + dot(hi_ref[:, at], ret_recv[at, :])
    gi_ref[:, :LANES] = low.astype(BF)
    gi_ref[:, LANES:] = high.astype(BF)

    sent = send_ref.at[pl.ds(0, (ring * wide - 1) * OUT)]
    pltpu.make_async_copy(sent, sent, a2a_s).wait()
    pltpu.make_async_copy(nsend_ref, nsend_ref, near_s).wait()
    sent = ret_send.at[pl.ds(0, (ne - 1) * BACK)]
    pltpu.make_async_copy(sent, sent, ret_s).wait()
    for way in range(2):
        for s in range(half - 1):
            sent = g_ref.at[0, pl.ds(0, ring * rows)]
            pltpu.make_async_copy(sent, sent, ag_s.at[way, s]).wait()
        for k in range(half):
            sent = rs_send.at[0, 0]
            if k == 0:
                sent = rs_send.at[0, 0, pl.ds(0, ny * (rows // 2))]
            pltpu.make_async_copy(sent, sent, rs_s.at[way, k]).wait()


def settle(*arrays):
    n = len(arrays)

    def body(*refs):
        for i in range(n):
            refs[n + i][...] = refs[i][...]

    vmem = pl.BlockSpec(memory_space=pltpu.VMEM)
    return pl.pallas_call(
        body,
        out_shape=tuple(jax.ShapeDtypeStruct(a.shape, a.dtype) for a in arrays),
        in_specs=[vmem] * n,
        out_specs=(vmem,) * n,
        compiler_params=pltpu.CompilerParams(vmem_limit_bytes=16 * 1024 * 1024),
    )(*arrays)


def tables(ne, side):
    wide = 2 * side
    gp = min(4, wide)
    perm = np.zeros((gp * OUT, gp * OUT), np.float32)
    for j in range(4):
        for s in range(gp):
            for r in range(CAP):
                perm[j * gp * CAP + s * CAP + r, s * OUT + j * CAP + r] = 1.0
    back = np.zeros((2, wide * BACK, wide * CAP), np.float32)
    for s in range(wide):
        for r in range(CAP):
            for m in range(2):
                back[m, s * BACK + m * CAP + r, s * CAP + r] = 1.0
    expand = np.kron(np.eye(ne, dtype=np.float32), np.ones((1, BACK), np.float32))
    phase = np.tile(np.arange(BACK, dtype=np.float32), ne)[None, :]
    half = ml_dtypes.bfloat16
    return gp, perm.astype(half), back.astype(half), expand.astype(half), phase


def solution(mesh):
    ne, nt = mesh.shape["expert"], mesh.shape["tensor"]
    side = SIDE
    wide = 2 * side
    ny, half = ne // wide, nt // 2
    rows = ne * CAP
    ring = ring_chunks(ny)
    direct = ny - ring
    gp, perm, back, expand, phase = tables(ne, side)

    def step(tokens, cotangent, expert_ids, gate_probs, w_gate, w_up, w_down):
        owned, width = tokens.shape
        vmem = pl.BlockSpec(memory_space=pltpu.VMEM)
        dma = pltpu.SemaphoreType.DMA
        gi, gg, gu, gd = pl.pallas_call(
            functools.partial(kernel, ne, nt, side, gp),
            out_shape=(
                jax.ShapeDtypeStruct((owned, PART), BF),
                jax.ShapeDtypeStruct((width, LANES), BF),
                jax.ShapeDtypeStruct((width, LANES), BF),
                jax.ShapeDtypeStruct((LANES, width), BF),
            ),
            in_specs=[vmem] * 11,
            out_specs=(vmem,) * 4,
            scratch_shapes=[
                pltpu.VMEM((ne, owned), F32),
                pltpu.VMEM((ne, owned), F32),
                pltpu.VMEM((4 * owned, 2 * LANES), BF),
                pltpu.VMEM((4 * owned, nt * LANES), BF),
                pltpu.VMEM((wide * OUT, 4 * owned), BF),
                pltpu.VMEM((ring * wide * OUT, 2 * LANES), BF),
                pltpu.VMEM((ring * wide * OUT, 2 * LANES), BF),
                pltpu.VMEM((direct * wide * OUT, nt * LANES), BF),
                pltpu.VMEM((direct * wide * OUT, nt * LANES), BF),
                pltpu.VMEM((nt, rows, 2 * PART), BF),
                pltpu.VMEM((width, 2 * LANES), BF),
                pltpu.VMEM((rows, 2 * LANES), BF),
                pltpu.VMEM((rows, LANES), BF),
                pltpu.VMEM((2, half, rows, PART), BF),
                pltpu.VMEM((2, half, rows, PART), BF),
                pltpu.VMEM((ne * BACK, LANES), BF),
                pltpu.VMEM((ne * BACK, LANES), BF),
                pltpu.VMEM((owned, ne * BACK), BF),
                pltpu.VMEM((owned, ne * BACK), BF),
                dma,
                dma,
                dma((ny,)),
                dma((2, half - 1)),
                dma((2, half - 1, ring)),
                dma((2, half)),
                dma((2, half, ny)),
                dma,
                dma((ny,)),
            ],
            compiler_params=pltpu.CompilerParams(
                collective_id=0, has_side_effects=True, vmem_limit_bytes=56 * 1024 * 1024
            ),
        )(
            expert_ids.T,
            gate_probs.T,
            tokens,
            cotangent,
            w_gate[0],
            w_up[0],
            w_down[0],
            jnp.asarray(perm),
            jnp.asarray(back),
            jnp.asarray(expand),
            jnp.asarray(phase),
        )
        gi, gg, gu, gd = settle(gi, gg, gu, gd)
        return gi, gg[None], gu[None], gd[None]

    return jax.shard_map(
        step,
        mesh=mesh,
        in_specs=(
            P("expert", None),
            P("expert", None),
            P("expert", None),
            P("expert", None),
            P("expert", None, "tensor"),
            P("expert", None, "tensor"),
            P("expert", "tensor", None),
        ),
        out_specs=(
            P("expert", "tensor"),
            P("expert", None, "tensor"),
            P("expert", None, "tensor"),
            P("expert", "tensor", None),
        ),
        check_vma=False,
    )
```

```python
import functools

import jax
import jax.numpy as jnp
import ml_dtypes
import numpy as np
from jax import lax
from jax.experimental import pallas as pl
from jax.experimental.pallas import tpu as pltpu
from jax.sharding import PartitionSpec as P

MESH = pl.DeviceIdType.MESH
BF = jnp.bfloat16
F32 = jnp.float32
CAP = 20
SIDE = 4
LANES = 128
PART = 256
OUT = 4 * CAP
BACK = 48
AHEAD = 1
LAG = 1


def ring_chunks(ny):
    return ny - 2 if ny > 4 else ny - 1


def dot(a, b):
    return jnp.dot(a, b, preferred_element_type=F32)


def dot_t(a, b):
    return lax.dot_general(a, b, (((1,), (1,)), ((), ())), preferred_element_type=F32)


def t_dot(a, b):
    return lax.dot_general(a, b, (((0,), (0,)), ((), ())), preferred_element_type=F32)


def kernel(
    ne, nt, side, gp,
    idst_ref, probst_ref, tok_ref, cot_ref, wg_hbm, wu_hbm, wd_hbm,
    perm_ref, back_hbm, expand_hbm, phase_ref,
    gi_ref, gg_ref, gu_ref, gd_ref,
    wd_ref, back_ref, expand_ref, key_ref, pr_ref, rhs_ref, all_ref, sel_ref, send_ref, recv_ref, nsend_ref, nrecv_ref, g_ref, w_ref, d_ref, sc_ref,
    rs_send, rs_recv, ret_send, ret_recv, lo_ref, hi_ref,
    a2a_s, near_s, a2a_r, ag_s, ag_r, rs_s, rs_r, ret_s, ret_r, load_s,
):
    wide = 2 * side
    ny = ne // wide
    half = nt // 2
    rows = wide * CAP
    ring = ring_chunks(ny)
    tokens = tok_ref.shape[0]
    ei, ti = lax.axis_index("expert"), lax.axis_index("tensor")
    yy, xx, core = ei // wide, lax.rem(ei // 2, side), lax.rem(ei, 2)
    right, left = lax.rem(ti + 1, nt), lax.rem(ti + nt - 1, nt)
    opp = lax.rem(ti + half, nt)

    def away(c):
        c = (lax.rem(c + 1, ny - 1) + 1) * jnp.minimum(c, 1)
        h, odd = (c + 1) // 2, lax.rem(c, 2)
        return odd * h + (1 - odd) * (ny - h)

    def row_to(c):
        return lax.rem(yy + 2 * ny - away(c), ny)

    def peer_to(c, s):
        dx, dc = s // 2, lax.rem(s, 2)
        return row_to(c) * wide + lax.rem(xx + side - dx, side) * 2 + lax.rem(core + dc, 2)

    def peer_from(c, s):
        dx, dc = s // 2, lax.rem(s, 2)
        return (
            lax.rem(yy + away(c), ny) * wide
            + lax.rem(xx + dx, side) * 2
            + lax.rem(core + dc, 2)
        )

    def turned(i):
        return lax.rem(i + core * (wide // 2), wide)

    def others(act):
        for s in range(1, wide):
            act(0, s)

        @pl.loop(1, ny)
        def _(c):
            for s in range(wide):
                act(c, s)

    loads = [
        pltpu.make_async_copy(src, dst, load_s.at[i])
        for i, (src, dst) in enumerate(
            (
                (wg_hbm, w_ref.at[:, pl.ds(0, LANES)]),
                (wu_hbm, w_ref.at[:, pl.ds(LANES, LANES)]),
                (wd_hbm, wd_ref),
                (back_hbm, back_ref),
                (expand_hbm, expand_ref),
            )
        )
    ]

    bar = pltpu.get_barrier_semaphore()
    others(
        lambda c, s: pl.semaphore_signal(
            bar, inc=1, device_id=(peer_to(c, s), ti), device_id_type=MESH
        )
    )
    for z in (right, left):
        pl.semaphore_signal(bar, inc=1, device_id=(ei, z), device_id_type=MESH)

    hits = jnp.zeros((ne, tokens), F32)
    prob = jnp.zeros((ne, tokens), F32)
    experts = lax.broadcasted_iota(jnp.int32, (ne, tokens), 0)
    given = probst_ref[...].astype(F32)
    for k in range(idst_ref.shape[0]):
        hit = idst_ref[k : k + 1, :] == experts
        hits = jnp.where(hit, 1.0, hits)
        prob = jnp.where(hit, given[k : k + 1, :], prob)
    r0 = lax.broadcasted_iota(jnp.int32, (tokens, tokens), 0)
    r1 = lax.broadcasted_iota(jnp.int32, (tokens, tokens), 1)
    before = jnp.where(r0 < r1, 1.0, 0.0).astype(BF)
    key_ref[...] = jnp.where(hits > 0.0, dot(hits.astype(BF), before), -1000.0)
    pr_ref[...] = prob

    for j in range(2):
        for m, start in enumerate((ti, opp)):
            at = pl.ds(pl.multiple_of(start * PART + j * LANES, LANES), LANES)
            cols = slice(m * LANES, (m + 1) * LANES)
            rhs_ref[j * tokens : (j + 1) * tokens, cols] = tok_ref[:, at]
            rhs_ref[(2 + j) * tokens : (3 + j) * tokens, cols] = cot_ref[:, at]

    def send_copy(c, s, near):
        to = peer_to(c, s)
        src, dst, first = (nsend_ref, nrecv_ref, ring) if near else (send_ref, recv_ref, 0)
        row = (c - first) * wide
        return pltpu.make_async_remote_copy(
            src_ref=src.at[
                pl.ds(pl.multiple_of((row + to - row_to(c) * wide) * OUT, OUT), OUT)
            ],
            dst_ref=dst.at[pl.ds(pl.multiple_of((row + s) * OUT, OUT), OUT)],
            send_sem=near_s if near else a2a_s,
            recv_sem=a2a_r.at[c],
            device_id=(to, ti),
            device_id_type=MESH,
        )

    def select(c):
        first = row_to(c) * wide
        keys = key_ref[pl.ds(pl.multiple_of(first, wide), wide), :]
        probs = pr_ref[pl.ds(pl.multiple_of(first, wide), wide), :]
        place = lax.broadcasted_iota(jnp.int32, (OUT, tokens), 0).astype(F32)
        for i in range(wide):
            key = jnp.broadcast_to(keys[i : i + 1, :], (OUT, tokens))
            share = jnp.broadcast_to(probs[i : i + 1, :], (OUT, tokens))
            for j in range(4):
                value = 1.0 if j < 2 else share
                sel_ref[i * OUT : (i + 1) * OUT, j * tokens : (j + 1) * tokens] = jnp.where(
                    place - float(CAP * j) == key, value, 0.0
                ).astype(BF)

    def far_rows(c):
        return pl.ds(pl.multiple_of(c * wide * OUT, OUT), wide * OUT)

    def pack(c):
        select(c)
        if isinstance(c, int) and c >= ring:
            nsend_ref[far_rows(c - ring), :] = dot(sel_ref[...], all_ref[...]).astype(BF)
        else:
            send_ref[far_rows(c), :] = dot(sel_ref[...], rhs_ref[...]).astype(BF)

    def send(chunks):
        for c in chunks:
            pack(c)
        for i in range(wide):
            for c in chunks:
                send_copy(c, turned(i), c >= ring).start()

    groups = [range(c, min(c + 2, ring)) for c in range(1, ring, 2)] + [range(ring, ny)]

    pack(0)
    mine = ei - yy * wide
    own = pltpu.make_async_copy(
        send_ref.at[pl.ds(pl.multiple_of(mine * OUT, OUT), OUT)],
        recv_ref.at[pl.ds(0, OUT)],
        a2a_r.at[0],
    )
    own.start()
    pl.semaphore_wait(bar, ne + 1)
    for s in range(1, wide):
        send_copy(0, s, False).start()

    for load in loads:
        load.start()
    for group in groups[:AHEAD]:
        send(group)
    for j in range(2):
        for u in range(nt):
            cols = slice(u * LANES, (u + 1) * LANES)
            at = slice(u * PART + j * LANES, u * PART + (j + 1) * LANES)
            all_ref[j * tokens : (j + 1) * tokens, cols] = tok_ref[:, at]
            all_ref[(2 + j) * tokens : (3 + j) * tokens, cols] = cot_ref[:, at]

    def prepare():
        for load in loads:
            load.wait()

    def block(c):
        return pl.ds(pl.multiple_of(c * rows, rows), rows)

    def ag_copy(c, s, way):
        unit = lax.rem(ti + nt - s, nt) if way == 0 else lax.rem(ti + s, nt)
        ref = g_ref.at[unit, block(c)]
        return pltpu.make_async_remote_copy(
            src_ref=ref,
            dst_ref=ref,
            send_sem=ag_s.at[way, s],
            recv_sem=ag_r.at[way, s, c],
            device_id=(ei, right if way == 0 else left),
            device_id_type=MESH,
        )

    def arrive(c):
        got = recv_ref.at[pl.ds(pl.multiple_of(c * wide * OUT, OUT), wide * OUT)]
        pltpu.make_async_copy(got, got, a2a_r.at[c]).wait()
        for g in range(wide // gp):
            at = pl.multiple_of((c * wide + g * gp) * OUT, OUT)
            out = dot(perm_ref[...], recv_ref[pl.ds(at, gp * OUT), :]).astype(BF)
            to = pl.ds(pl.multiple_of(c * rows + g * gp * CAP, gp * CAP), gp * CAP)
            for j in range(4):
                piece = out[j * gp * CAP : (j + 1) * gp * CAP, :]
                g_ref[ti, to, j * LANES : (j + 1) * LANES] = piece[:, :LANES]
                g_ref[opp, to, j * LANES : (j + 1) * LANES] = piece[:, LANES:]
        for way in range(2):
            ag_copy(c, 0, way).start()

    def direct(c):
        got = nrecv_ref.at[far_rows(c - ring)]
        pltpu.make_async_copy(got, got, a2a_r.at[c]).wait()
        for g in range(wide // gp):
            at = pl.multiple_of(((c - ring) * wide + g * gp) * OUT, OUT)
            to = pl.ds(pl.multiple_of(c * rows + g * gp * CAP, gp * CAP), gp * CAP)
            for u in range(0, nt, 2):
                cols = slice(u * LANES, (u + 2) * LANES)
                out = dot(perm_ref[...], nrecv_ref[pl.ds(at, gp * OUT), cols]).astype(BF)
                for j in range(4):
                    piece = out[j * gp * CAP : (j + 1) * gp * CAP, :]
                    g_ref[u, to, j * LANES : (j + 1) * LANES] = piece[:, :LANES]
                    g_ref[u + 1, to, j * LANES : (j + 1) * LANES] = piece[:, LANES:]
        hidden(c)

    def ag_wait(c, s):
        for way in range(2):
            unit = lax.rem(ti + nt - s - 1, nt) if way == 0 else lax.rem(ti + s + 1, nt)
            ref = g_ref.at[unit, block(c)]
            pltpu.make_async_copy(ref, ref, ag_r.at[way, s, c]).wait()

    def forward(s, c):
        ag_wait(c, s - 1)
        for way in range(2):
            ag_copy(c, s, way).start()

    def piece_of(c, target):
        at = pl.ds(pl.multiple_of(target * PART, PART), PART)
        return dot_t(d_ref[block(c), :], w_ref[at, :])

    def rs_rows(c, k, way):
        if k > 0:
            return block(c)
        return pl.ds(pl.multiple_of(c * rows + way * (rows // 2), rows // 2), rows // 2)

    def rs_copy(c, k, way):
        at = rs_rows(c, k, way)
        return pltpu.make_async_remote_copy(
            src_ref=rs_send.at[0 if k == 0 else way, k, at],
            dst_ref=rs_recv.at[way, k, at],
            send_sem=rs_s.at[way, k],
            recv_sem=rs_r.at[way, k, c],
            device_id=(ei, right if way == 0 else left),
            device_id_type=MESH,
        )

    def rs_wait(c, k, way):
        ref = rs_recv.at[way, k, rs_rows(c, k, way)]
        pltpu.make_async_copy(ref, ref, rs_r.at[way, k, c]).wait()

    def middle(c):
        ag_wait(c, half - 2)
        hidden(c)

    def hidden(c):
        at = block(c)
        both = jnp.zeros((rows, 2 * LANES), F32)
        dhid = jnp.zeros((rows, LANES), F32)
        for u in range(nt):
            cols = slice(u * PART, (u + 1) * PART)
            both = both + dot(g_ref[u, at, :PART], w_ref[cols, :])
            dhid = dhid + dot_t(g_ref[u, at, PART:], wd_ref[:, cols])
        gate, upper = both[:, :LANES], both[:, LANES:]
        sig = 1.0 / (1.0 + jnp.exp(-gate))
        act = gate * sig
        sc_ref[at, :] = (act * upper).astype(BF)
        d_ref[at, :LANES] = (dhid * upper * sig * (1.0 + gate * (1.0 - sig))).astype(BF)
        d_ref[at, LANES:] = (dhid * act).astype(BF)
        rs_send[0, 0, at, :] = piece_of(c, opp).astype(BF)
        for way in range(2):
            rs_copy(c, 0, way).start()

    def add(k, c):
        for way in range(2):
            hop = half - k
            target = lax.rem(ti + hop, nt) if way == 0 else lax.rem(ti + nt - hop, nt)
            piece = piece_of(c, target)
            rs_wait(c, k - 1, way)
            if k > 1:
                got = rs_recv[way, k - 1, block(c), :].astype(F32)
                rs_send[way, k, block(c), :] = (piece + got).astype(BF)
            else:
                for part in range(2):
                    at = rs_rows(c, 0, part)
                    here = piece[part * (rows // 2) : (part + 1) * (rows // 2), :]
                    if part == way:
                        here = here + rs_recv[way, 0, at, :].astype(F32)
                    rs_send[way, k, at, :] = here.astype(BF)
            rs_copy(c, k, way).start()

    def back_copy(c, s):
        return pltpu.make_async_remote_copy(
            src_ref=ret_send.at[pl.ds(pl.multiple_of((c * wide + s) * BACK, BACK), BACK)],
            dst_ref=ret_recv.at[pl.ds(pl.multiple_of(ei * BACK, BACK), BACK)],
            send_sem=ret_s,
            recv_sem=ret_r.at[c],
            device_id=(peer_from(c, s), ti),
            device_id_type=MESH,
        )

    def finish(c):
        piece = piece_of(c, ti)
        for way in range(2):
            rs_wait(c, half - 1, way)
            piece = piece + rs_recv[way, half - 1, block(c), :].astype(F32)
        whole = piece.astype(BF)
        at = pl.ds(pl.multiple_of(c * wide * BACK, BACK), wide * BACK)
        ret_send[at, :] = (
            dot(back_ref[0], whole[:, :LANES]) + dot(back_ref[1], whole[:, LANES:])
        ).astype(BF)

        @pl.when(c == 0)
        def _():
            pltpu.make_async_copy(
                ret_send.at[pl.ds(0, BACK)],
                ret_recv.at[pl.ds(pl.multiple_of(ei * BACK, BACK), BACK)],
                ret_r.at[c],
            ).start()
            for s in range(1, wide):
                back_copy(c, s).start()

        @pl.when(c != 0)
        def _():
            for i in range(wide):
                back_copy(c, turned(i)).start()

    def weight_grads(u):
        at = pl.ds(pl.multiple_of(u * PART, PART), PART)
        both = t_dot(g_ref[u, :, :PART], d_ref[...]).astype(BF)
        gg_ref[at, :] = both[:, :LANES]
        gu_ref[at, :] = both[:, LANES:]
        gd_ref[:, at] = t_dot(sc_ref[...], g_ref[u, :, PART:]).astype(BF)

    sums = [functools.partial(add, k) for k in range(1, half)] + [finish]
    stages = [arrive] + [functools.partial(forward, s) for s in range(1, half - 1)]
    stages += [middle] + sums

    def places():
        e0 = lax.broadcasted_iota(jnp.int32, (ne, ne), 0)
        e1 = lax.broadcasted_iota(jnp.int32, (ne, ne), 1)
        hits_n = t_dot(hits.astype(BF), jnp.where(e0 == e1, 1.0, 0.0).astype(BF))
        after = jnp.where(r1 < r0, 1.0, 0.0).astype(BF)
        key_n = jnp.where(hits_n > 0.0, dot(after, hits_n.astype(BF)), 200.0).astype(BF)
        tile = min(ne * BACK, 512)
        for n in range(0, ne * BACK, tile):
            want = dot(key_n, expand_ref[:, n : n + tile])
            phase = phase_ref[:, n : n + tile]
            lo_ref[:, n : n + tile] = jnp.where(want == phase, 1.0, 0.0).astype(BF)
            hi_ref[:, n : n + tile] = jnp.where(want + float(CAP) == phase, 1.0, 0.0).astype(BF)

    turns = max(ring - 1 + len(stages), ny - 1 + LAG + len(sums) + 1)
    last = max(ring + half - 1, ny + LAG)
    each = -(-nt // (turns - last))

    @pl.loop(0, turns)
    def _(turn):
        for i, group in enumerate(groups[AHEAD:]):
            pl.when(turn == i)(functools.partial(send, group))
        for i, stage in enumerate(stages):
            c = turn - i
            pl.when(jnp.logical_and(c >= 0, c < ring))(functools.partial(stage, c))
            if i == 0:
                pl.when(turn == 0)(prepare)
                pl.when(turn == 1)(places)
        for i, stage in enumerate([direct] + sums):
            c = turn - i - LAG
            pl.when(jnp.logical_and(c >= ring, c < ny))(functools.partial(stage, c))
        for i in range(each):
            u = (turn - last) * each + i
            pl.when(jnp.logical_and(turn >= last, u < nt))(functools.partial(weight_grads, u))

    low = jnp.zeros((tokens, LANES), F32)
    high = jnp.zeros((tokens, LANES), F32)
    for c in range(ny):
        at = pl.ds(pl.multiple_of(row_to(c) * wide * BACK, wide * BACK), wide * BACK)
        got = ret_recv.at[at]
        pltpu.make_async_copy(got, got, ret_r.at[c]).wait()
        low = low + dot(lo_ref[:, at], ret_recv[at, :])
        high = high + dot(hi_ref[:, at], ret_recv[at, :])
    gi_ref[:, :LANES] = low.astype(BF)
    gi_ref[:, LANES:] = high.astype(BF)

    sent = send_ref.at[pl.ds(0, (ring * wide - 1) * OUT)]
    pltpu.make_async_copy(sent, sent, a2a_s).wait()
    pltpu.make_async_copy(nsend_ref, nsend_ref, near_s).wait()
    sent = ret_send.at[pl.ds(0, (ne - 1) * BACK)]
    pltpu.make_async_copy(sent, sent, ret_s).wait()
    for way in range(2):
        for s in range(half - 1):
            sent = g_ref.at[0, pl.ds(0, ring * rows)]
            pltpu.make_async_copy(sent, sent, ag_s.at[way, s]).wait()
        for k in range(half):
            sent = rs_send.at[0, 0]
            if k == 0:
                sent = rs_send.at[0, 0, pl.ds(0, ny * (rows // 2))]
            pltpu.make_async_copy(sent, sent, rs_s.at[way, k]).wait()


def settle(*arrays):
    n = len(arrays)

    def body(*refs):
        here, sems = refs[2 * n : 3 * n], refs[3 * n]
        ins = [pltpu.make_async_copy(refs[i], here[i], sems.at[0, i]) for i in range(n)]
        outs = [pltpu.make_async_copy(here[i], refs[n + i], sems.at[1, i]) for i in range(n)]
        for copy in ins:
            copy.start()
        for i in range(n):
            ins[i].wait()
            outs[i].start()
        for copy in outs:
            copy.wait()

    any_space = pl.BlockSpec(memory_space=pl.ANY)
    return pl.pallas_call(
        body,
        out_shape=tuple(jax.ShapeDtypeStruct(a.shape, a.dtype) for a in arrays),
        in_specs=[any_space] * n,
        out_specs=(any_space,) * n,
        scratch_shapes=[pltpu.VMEM(a.shape, a.dtype) for a in arrays]
        + [pltpu.SemaphoreType.DMA((2, n))],
        compiler_params=pltpu.CompilerParams(vmem_limit_bytes=56 * 1024 * 1024),
    )(*arrays)


def tables(ne, side):
    wide = 2 * side
    gp = min(4, wide)
    perm = np.zeros((gp * OUT, gp * OUT), np.float32)
    for j in range(4):
        for s in range(gp):
            for r in range(CAP):
                perm[j * gp * CAP + s * CAP + r, s * OUT + j * CAP + r] = 1.0
    back = np.zeros((2, wide * BACK, wide * CAP), np.float32)
    for s in range(wide):
        for r in range(CAP):
            for m in range(2):
                back[m, s * BACK + m * CAP + r, s * CAP + r] = 1.0
    expand = np.kron(np.eye(ne, dtype=np.float32), np.ones((1, BACK), np.float32))
    phase = np.tile(np.arange(BACK, dtype=np.float32), ne)[None, :]
    half = ml_dtypes.bfloat16
    return gp, perm.astype(half), back.astype(half), expand.astype(half), phase


def solution(mesh):
    ne, nt = mesh.shape["expert"], mesh.shape["tensor"]
    side = SIDE
    wide = 2 * side
    ny, half = ne // wide, nt // 2
    rows = ne * CAP
    ring = ring_chunks(ny)
    direct = ny - ring
    gp, perm, back, expand, phase = tables(ne, side)

    def step(tokens, cotangent, expert_ids, gate_probs, w_gate, w_up, w_down):
        owned, width = tokens.shape
        vmem = pl.BlockSpec(memory_space=pltpu.VMEM)
        hbm = pl.BlockSpec(memory_space=pl.ANY)
        dma = pltpu.SemaphoreType.DMA
        gi, gg, gu, gd = pl.pallas_call(
            functools.partial(kernel, ne, nt, side, gp),
            out_shape=(
                jax.ShapeDtypeStruct((owned, PART), BF),
                jax.ShapeDtypeStruct((width, LANES), BF),
                jax.ShapeDtypeStruct((width, LANES), BF),
                jax.ShapeDtypeStruct((LANES, width), BF),
            ),
            in_specs=[vmem] * 4 + [hbm] * 3 + [vmem] + [hbm] * 2 + [vmem],
            out_specs=(vmem,) * 4,
            scratch_shapes=[
                pltpu.VMEM((LANES, width), BF),
                pltpu.VMEM(back.shape, BF),
                pltpu.VMEM(expand.shape, BF),
                pltpu.VMEM((ne, owned), F32),
                pltpu.VMEM((ne, owned), F32),
                pltpu.VMEM((4 * owned, 2 * LANES), BF),
                pltpu.VMEM((4 * owned, nt * LANES), BF),
                pltpu.VMEM((wide * OUT, 4 * owned), BF),
                pltpu.VMEM((ring * wide * OUT, 2 * LANES), BF),
                pltpu.VMEM((ring * wide * OUT, 2 * LANES), BF),
                pltpu.VMEM((direct * wide * OUT, nt * LANES), BF),
                pltpu.VMEM((direct * wide * OUT, nt * LANES), BF),
                pltpu.VMEM((nt, rows, 2 * PART), BF),
                pltpu.VMEM((width, 2 * LANES), BF),
                pltpu.VMEM((rows, 2 * LANES), BF),
                pltpu.VMEM((rows, LANES), BF),
                pltpu.VMEM((2, half, rows, PART), BF),
                pltpu.VMEM((2, half, rows, PART), BF),
                pltpu.VMEM((ne * BACK, LANES), BF),
                pltpu.VMEM((ne * BACK, LANES), BF),
                pltpu.VMEM((owned, ne * BACK), BF),
                pltpu.VMEM((owned, ne * BACK), BF),
                dma,
                dma,
                dma((ny,)),
                dma((2, half - 1)),
                dma((2, half - 1, ring)),
                dma((2, half)),
                dma((2, half, ny)),
                dma,
                dma((ny,)),
                dma((5,)),
            ],
            compiler_params=pltpu.CompilerParams(
                collective_id=0, has_side_effects=True, vmem_limit_bytes=56 * 1024 * 1024
            ),
        )(
            expert_ids.T,
            gate_probs.T,
            tokens,
            cotangent,
            w_gate[0],
            w_up[0],
            w_down[0],
            jnp.asarray(perm),
            jnp.asarray(back),
            jnp.asarray(expand),
            jnp.asarray(phase),
        )
        gi, gg, gu, gd = settle(gi, gg, gu, gd)
        return gi, gg[None], gu[None], gd[None]

    return jax.shard_map(
        step,
        mesh=mesh,
        in_specs=(
            P("expert", None),
            P("expert", None),
            P("expert", None),
            P("expert", None),
            P("expert", None, "tensor"),
            P("expert", None, "tensor"),
            P("expert", "tensor", None),
        ),
        out_specs=(
            P("expert", "tensor"),
            P("expert", None, "tensor"),
            P("expert", None, "tensor"),
            P("expert", "tensor", None),
        ),
        check_vma=False,
    )
```

```python
import functools

import jax
import jax.numpy as jnp
import ml_dtypes
import numpy as np
from jax import lax
from jax.experimental import pallas as pl
from jax.experimental.pallas import tpu as pltpu
from jax.sharding import PartitionSpec as P

MESH = pl.DeviceIdType.MESH
BF = jnp.bfloat16
F32 = jnp.float32
CAP = 20
SIDE = 4
LANES = 128
PART = 256
OUT = 4 * CAP
BACK = 48
AHEAD = 1
LAG = 1


def ring_chunks(ny):
    return ny - 2 if ny > 4 else ny - 1


def dot(a, b):
    return jnp.dot(a, b, preferred_element_type=F32)


def dot_t(a, b):
    return lax.dot_general(a, b, (((1,), (1,)), ((), ())), preferred_element_type=F32)


def t_dot(a, b):
    return lax.dot_general(a, b, (((0,), (0,)), ((), ())), preferred_element_type=F32)


def kernel(
    ne, nt, side, gp,
    idst_ref, probst_ref, tok_ref, cot_ref, wg_hbm, wu_hbm, wd_hbm,
    perm_ref, back_hbm, expand_hbm, phase_ref,
    gi_ref, gg_ref, gu_ref, gd_ref,
    wd_ref, back_ref, expand_ref, key_ref, pr_ref, rhs_ref, all_ref, sel_ref, send_ref, recv_ref, nsend_ref, nrecv_ref, g_ref, w_ref, d_ref, sc_ref,
    rs_send, rs_recv, ret_send, ret_recv, lo_ref, hi_ref,
    a2a_s, near_s, a2a_r, ag_s, ag_r, rs_s, rs_r, ret_s, ret_r, load_s,
):
    wide = 2 * side
    ny = ne // wide
    half = nt // 2
    rows = wide * CAP
    ring = ring_chunks(ny)
    tokens = tok_ref.shape[0]
    ei, ti = lax.axis_index("expert"), lax.axis_index("tensor")
    yy, xx, core = ei // wide, lax.rem(ei // 2, side), lax.rem(ei, 2)
    right, left = lax.rem(ti + 1, nt), lax.rem(ti + nt - 1, nt)
    opp = lax.rem(ti + half, nt)

    def away(c):
        c = (lax.rem(c + 1, ny - 1) + 1) * jnp.minimum(c, 1)
        h, odd = (c + 1) // 2, lax.rem(c, 2)
        return odd * h + (1 - odd) * (ny - h)

    def row_to(c):
        return lax.rem(yy + 2 * ny - away(c), ny)

    def peer_to(c, s):
        dx, dc = s // 2, lax.rem(s, 2)
        return row_to(c) * wide + lax.rem(xx + side - dx, side) * 2 + lax.rem(core + dc, 2)

    def peer_from(c, s):
        dx, dc = s // 2, lax.rem(s, 2)
        return (
            lax.rem(yy + away(c), ny) * wide
            + lax.rem(xx + dx, side) * 2
            + lax.rem(core + dc, 2)
        )

    def turned(i):
        return lax.rem(i + core * (wide // 2), wide)

    def others(act):
        for s in range(1, wide):
            act(0, s)

        @pl.loop(1, ny)
        def _(c):
            for s in range(wide):
                act(c, s)

    loads = [
        pltpu.make_async_copy(src, dst, load_s.at[i])
        for i, (src, dst) in enumerate(
            (
                (wg_hbm, w_ref.at[:, pl.ds(0, LANES)]),
                (wu_hbm, w_ref.at[:, pl.ds(LANES, LANES)]),
                (wd_hbm, wd_ref),
                (back_hbm, back_ref),
                (expand_hbm, expand_ref),
            )
        )
    ]

    bar = pltpu.get_barrier_semaphore()
    others(
        lambda c, s: pl.semaphore_signal(
            bar, inc=1, device_id=(peer_to(c, s), ti), device_id_type=MESH
        )
    )
    for z in (right, left):
        pl.semaphore_signal(bar, inc=1, device_id=(ei, z), device_id_type=MESH)

    hits = jnp.zeros((ne, tokens), F32)
    prob = jnp.zeros((ne, tokens), F32)
    experts = lax.broadcasted_iota(jnp.int32, (ne, tokens), 0)
    given = probst_ref[...].astype(F32)
    for k in range(idst_ref.shape[0]):
        hit = idst_ref[k : k + 1, :] == experts
        hits = jnp.where(hit, 1.0, hits)
        prob = jnp.where(hit, given[k : k + 1, :], prob)
    r0 = lax.broadcasted_iota(jnp.int32, (tokens, tokens), 0)
    r1 = lax.broadcasted_iota(jnp.int32, (tokens, tokens), 1)
    before = jnp.where(r0 < r1, 1.0, 0.0).astype(BF)
    key_ref[...] = jnp.where(hits > 0.0, dot(hits.astype(BF), before), -1000.0)
    pr_ref[...] = prob

    for j in range(2):
        for m, start in enumerate((ti, opp)):
            at = pl.ds(pl.multiple_of(start * PART + j * LANES, LANES), LANES)
            cols = slice(m * LANES, (m + 1) * LANES)
            rhs_ref[j * tokens : (j + 1) * tokens, cols] = tok_ref[:, at]
            rhs_ref[(2 + j) * tokens : (3 + j) * tokens, cols] = cot_ref[:, at]

    def send_copy(c, s, near):
        to = peer_to(c, s)
        src, dst, first = (nsend_ref, nrecv_ref, ring) if near else (send_ref, recv_ref, 0)
        row = (c - first) * wide
        return pltpu.make_async_remote_copy(
            src_ref=src.at[
                pl.ds(pl.multiple_of((row + to - row_to(c) * wide) * OUT, OUT), OUT)
            ],
            dst_ref=dst.at[pl.ds(pl.multiple_of((row + s) * OUT, OUT), OUT)],
            send_sem=near_s if near else a2a_s,
            recv_sem=a2a_r.at[c],
            device_id=(to, ti),
            device_id_type=MESH,
        )

    def select(c):
        first = row_to(c) * wide
        keys = key_ref[pl.ds(pl.multiple_of(first, wide), wide), :]
        probs = pr_ref[pl.ds(pl.multiple_of(first, wide), wide), :]
        place = lax.broadcasted_iota(jnp.int32, (OUT, tokens), 0).astype(F32)
        for i in range(wide):
            key = jnp.broadcast_to(keys[i : i + 1, :], (OUT, tokens))
            share = jnp.broadcast_to(probs[i : i + 1, :], (OUT, tokens))
            for j in range(4):
                value = 1.0 if j < 2 else share
                sel_ref[i * OUT : (i + 1) * OUT, j * tokens : (j + 1) * tokens] = jnp.where(
                    place - float(CAP * j) == key, value, 0.0
                ).astype(BF)

    def far_rows(c):
        return pl.ds(pl.multiple_of(c * wide * OUT, OUT), wide * OUT)

    def pack(c):
        select(c)
        if isinstance(c, int) and c >= ring:
            nsend_ref[far_rows(c - ring), :] = dot(sel_ref[...], all_ref[...]).astype(BF)
        else:
            send_ref[far_rows(c), :] = dot(sel_ref[...], rhs_ref[...]).astype(BF)

    def send(chunks):
        for c in chunks:
            pack(c)
        for i in range(wide):
            for c in chunks:
                send_copy(c, turned(i), c >= ring).start()

    groups = [range(c, min(c + 2, ring)) for c in range(1, ring, 2)] + [range(ring, ny)]

    pack(0)
    mine = ei - yy * wide
    own = pltpu.make_async_copy(
        send_ref.at[pl.ds(pl.multiple_of(mine * OUT, OUT), OUT)],
        recv_ref.at[pl.ds(0, OUT)],
        a2a_r.at[0],
    )
    own.start()
    pl.semaphore_wait(bar, ne + 1)
    for s in range(1, wide):
        send_copy(0, s, False).start()

    for load in loads:
        load.start()
    for group in groups[:AHEAD]:
        send(group)
    for j in range(2):
        for u in range(nt):
            cols = slice(u * LANES, (u + 1) * LANES)
            at = slice(u * PART + j * LANES, u * PART + (j + 1) * LANES)
            all_ref[j * tokens : (j + 1) * tokens, cols] = tok_ref[:, at]
            all_ref[(2 + j) * tokens : (3 + j) * tokens, cols] = cot_ref[:, at]

    def prepare():
        for load in loads:
            load.wait()

    def block(c):
        return pl.ds(pl.multiple_of(c * rows, rows), rows)

    def ag_copy(c, s, way):
        unit = lax.rem(ti + nt - s, nt) if way == 0 else lax.rem(ti + s, nt)
        ref = g_ref.at[unit, block(c)]
        return pltpu.make_async_remote_copy(
            src_ref=ref,
            dst_ref=ref,
            send_sem=ag_s.at[way, s],
            recv_sem=ag_r.at[way, s, c],
            device_id=(ei, right if way == 0 else left),
            device_id_type=MESH,
        )

    def arrive(c):
        got = recv_ref.at[pl.ds(pl.multiple_of(c * wide * OUT, OUT), wide * OUT)]
        pltpu.make_async_copy(got, got, a2a_r.at[c]).wait()
        for g in range(wide // gp):
            at = pl.multiple_of((c * wide + g * gp) * OUT, OUT)
            out = dot(perm_ref[...], recv_ref[pl.ds(at, gp * OUT), :]).astype(BF)
            to = pl.ds(pl.multiple_of(c * rows + g * gp * CAP, gp * CAP), gp * CAP)
            for j in range(4):
                piece = out[j * gp * CAP : (j + 1) * gp * CAP, :]
                g_ref[ti, to, j * LANES : (j + 1) * LANES] = piece[:, :LANES]
                g_ref[opp, to, j * LANES : (j + 1) * LANES] = piece[:, LANES:]
        for way in range(2):
            ag_copy(c, 0, way).start()

    def direct(c):
        got = nrecv_ref.at[far_rows(c - ring)]
        pltpu.make_async_copy(got, got, a2a_r.at[c]).wait()
        for g in range(wide // gp):
            at = pl.multiple_of(((c - ring) * wide + g * gp) * OUT, OUT)
            to = pl.ds(pl.multiple_of(c * rows + g * gp * CAP, gp * CAP), gp * CAP)
            for u in range(0, nt, 2):
                cols = slice(u * LANES, (u + 2) * LANES)
                out = dot(perm_ref[...], nrecv_ref[pl.ds(at, gp * OUT), cols]).astype(BF)
                for j in range(4):
                    piece = out[j * gp * CAP : (j + 1) * gp * CAP, :]
                    g_ref[u, to, j * LANES : (j + 1) * LANES] = piece[:, :LANES]
                    g_ref[u + 1, to, j * LANES : (j + 1) * LANES] = piece[:, LANES:]
        hidden(c)

    def ag_wait(c, s):
        for way in range(2):
            unit = lax.rem(ti + nt - s - 1, nt) if way == 0 else lax.rem(ti + s + 1, nt)
            ref = g_ref.at[unit, block(c)]
            pltpu.make_async_copy(ref, ref, ag_r.at[way, s, c]).wait()

    def forward(s, c):
        ag_wait(c, s - 1)
        for way in range(2):
            ag_copy(c, s, way).start()

    def piece_of(c, target):
        at = pl.ds(pl.multiple_of(target * PART, PART), PART)
        return dot_t(d_ref[block(c), :], w_ref[at, :])

    def rs_rows(c, k, way):
        if k > 0:
            return block(c)
        return pl.ds(pl.multiple_of(c * rows + way * (rows // 2), rows // 2), rows // 2)

    def rs_copy(c, k, way):
        at = rs_rows(c, k, way)
        return pltpu.make_async_remote_copy(
            src_ref=rs_send.at[0 if k == 0 else way, k, at],
            dst_ref=rs_recv.at[way, k, at],
            send_sem=rs_s.at[way, k],
            recv_sem=rs_r.at[way, k, c],
            device_id=(ei, right if way == 0 else left),
            device_id_type=MESH,
        )

    def rs_wait(c, k, way):
        ref = rs_recv.at[way, k, rs_rows(c, k, way)]
        pltpu.make_async_copy(ref, ref, rs_r.at[way, k, c]).wait()

    def middle(c):
        ag_wait(c, half - 2)
        hidden(c)

    def hidden(c):
        at = block(c)
        both = jnp.zeros((rows, 2 * LANES), F32)
        dhid = jnp.zeros((rows, LANES), F32)
        for u in range(nt):
            cols = slice(u * PART, (u + 1) * PART)
            both = both + dot(g_ref[u, at, :PART], w_ref[cols, :])
            dhid = dhid + dot_t(g_ref[u, at, PART:], wd_ref[:, cols])
        gate, upper = both[:, :LANES], both[:, LANES:]
        sig = 1.0 / (1.0 + jnp.exp(-gate))
        act = gate * sig
        sc_ref[at, :] = (act * upper).astype(BF)
        d_ref[at, :LANES] = (dhid * upper * sig * (1.0 + gate * (1.0 - sig))).astype(BF)
        d_ref[at, LANES:] = (dhid * act).astype(BF)
        rs_send[0, 0, at, :] = piece_of(c, opp).astype(BF)
        for way in range(2):
            rs_copy(c, 0, way).start()

    def add(k, c):
        for way in range(2):
            hop = half - k
            target = lax.rem(ti + hop, nt) if way == 0 else lax.rem(ti + nt - hop, nt)
            piece = piece_of(c, target)
            rs_wait(c, k - 1, way)
            if k > 1:
                got = rs_recv[way, k - 1, block(c), :].astype(F32)
                rs_send[way, k, block(c), :] = (piece + got).astype(BF)
            else:
                for part in range(2):
                    at = rs_rows(c, 0, part)
                    here = piece[part * (rows // 2) : (part + 1) * (rows // 2), :]
                    if part == way:
                        here = here + rs_recv[way, 0, at, :].astype(F32)
                    rs_send[way, k, at, :] = here.astype(BF)
            rs_copy(c, k, way).start()

    def back_copy(c, s):
        return pltpu.make_async_remote_copy(
            src_ref=ret_send.at[pl.ds(pl.multiple_of((c * wide + s) * BACK, BACK), BACK)],
            dst_ref=ret_recv.at[pl.ds(pl.multiple_of(ei * BACK, BACK), BACK)],
            send_sem=ret_s,
            recv_sem=ret_r.at[c],
            device_id=(peer_from(c, s), ti),
            device_id_type=MESH,
        )

    def finish(c):
        piece = piece_of(c, ti)
        for way in range(2):
            rs_wait(c, half - 1, way)
            piece = piece + rs_recv[way, half - 1, block(c), :].astype(F32)
        whole = piece.astype(BF)
        at = pl.ds(pl.multiple_of(c * wide * BACK, BACK), wide * BACK)
        ret_send[at, :] = (
            dot(back_ref[0], whole[:, :LANES]) + dot(back_ref[1], whole[:, LANES:])
        ).astype(BF)

        @pl.when(c == 0)
        def _():
            pltpu.make_async_copy(
                ret_send.at[pl.ds(0, BACK)],
                ret_recv.at[pl.ds(pl.multiple_of(ei * BACK, BACK), BACK)],
                ret_r.at[c],
            ).start()
            for s in range(1, wide):
                back_copy(c, s).start()

        @pl.when(c != 0)
        def _():
            for i in range(wide):
                back_copy(c, turned(i)).start()

    def weight_grads(u):
        at = pl.ds(pl.multiple_of(u * PART, PART), PART)
        both = t_dot(g_ref[u, :, :PART], d_ref[...]).astype(BF)
        gg_ref[at, :] = both[:, :LANES]
        gu_ref[at, :] = both[:, LANES:]
        gd_ref[:, at] = t_dot(sc_ref[...], g_ref[u, :, PART:]).astype(BF)

    sums = [functools.partial(add, k) for k in range(1, half)] + [finish]
    stages = [arrive] + [functools.partial(forward, s) for s in range(1, half - 1)]
    stages += [middle] + sums

    def places():
        e0 = lax.broadcasted_iota(jnp.int32, (ne, ne), 0)
        e1 = lax.broadcasted_iota(jnp.int32, (ne, ne), 1)
        hits_n = t_dot(hits.astype(BF), jnp.where(e0 == e1, 1.0, 0.0).astype(BF))
        after = jnp.where(r1 < r0, 1.0, 0.0).astype(BF)
        key_n = jnp.where(hits_n > 0.0, dot(after, hits_n.astype(BF)), 200.0).astype(BF)
        tile = min(ne * BACK, 512)
        for n in range(0, ne * BACK, tile):
            want = dot(key_n, expand_ref[:, n : n + tile])
            phase = phase_ref[:, n : n + tile]
            lo_ref[:, n : n + tile] = jnp.where(want == phase, 1.0, 0.0).astype(BF)
            hi_ref[:, n : n + tile] = jnp.where(want + float(CAP) == phase, 1.0, 0.0).astype(BF)

    turns = max(ring - 1 + len(stages), ny - 1 + LAG + len(sums) + 1)
    last = max(ring + half - 1, ny + LAG)
    each = -(-nt // (turns - last))

    @pl.loop(0, turns)
    def _(turn):
        for i, stage in reversed(list(enumerate(stages))[1:]):
            c = turn - i
            pl.when(jnp.logical_and(c >= 0, c < ring))(functools.partial(stage, c))
        for i, stage in reversed(list(enumerate([direct] + sums))):
            c = turn - i - LAG
            pl.when(jnp.logical_and(c >= ring, c < ny))(functools.partial(stage, c))
        pl.when(turn < ring)(functools.partial(arrive, turn))

        @pl.when(turn == 0)
        def _():
            for group in groups[AHEAD:]:
                send(group)
            prepare()
            places()

        for i in range(each):
            u = (turn - last) * each + i
            pl.when(jnp.logical_and(turn >= last, u < nt))(functools.partial(weight_grads, u))

    low = jnp.zeros((tokens, LANES), F32)
    high = jnp.zeros((tokens, LANES), F32)
    for c in range(ny):
        at = pl.ds(pl.multiple_of(row_to(c) * wide * BACK, wide * BACK), wide * BACK)
        got = ret_recv.at[at]
        pltpu.make_async_copy(got, got, ret_r.at[c]).wait()
        low = low + dot(lo_ref[:, at], ret_recv[at, :])
        high = high + dot(hi_ref[:, at], ret_recv[at, :])
    gi_ref[:, :LANES] = low.astype(BF)
    gi_ref[:, LANES:] = high.astype(BF)

    sent = send_ref.at[pl.ds(0, (ring * wide - 1) * OUT)]
    pltpu.make_async_copy(sent, sent, a2a_s).wait()
    pltpu.make_async_copy(nsend_ref, nsend_ref, near_s).wait()
    sent = ret_send.at[pl.ds(0, (ne - 1) * BACK)]
    pltpu.make_async_copy(sent, sent, ret_s).wait()
    for way in range(2):
        for s in range(half - 1):
            sent = g_ref.at[0, pl.ds(0, ring * rows)]
            pltpu.make_async_copy(sent, sent, ag_s.at[way, s]).wait()
        for k in range(half):
            sent = rs_send.at[0, 0]
            if k == 0:
                sent = rs_send.at[0, 0, pl.ds(0, ny * (rows // 2))]
            pltpu.make_async_copy(sent, sent, rs_s.at[way, k]).wait()


def settle(*arrays):
    n = len(arrays)

    def body(*refs):
        here, sems = refs[2 * n : 3 * n], refs[3 * n]
        ins = [pltpu.make_async_copy(refs[i], here[i], sems.at[0, i]) for i in range(n)]
        outs = [pltpu.make_async_copy(here[i], refs[n + i], sems.at[1, i]) for i in range(n)]
        for copy in ins:
            copy.start()
        for i in range(n):
            ins[i].wait()
            outs[i].start()
        for copy in outs:
            copy.wait()

    any_space = pl.BlockSpec(memory_space=pl.ANY)
    return pl.pallas_call(
        body,
        out_shape=tuple(jax.ShapeDtypeStruct(a.shape, a.dtype) for a in arrays),
        in_specs=[any_space] * n,
        out_specs=(any_space,) * n,
        scratch_shapes=[pltpu.VMEM(a.shape, a.dtype) for a in arrays]
        + [pltpu.SemaphoreType.DMA((2, n))],
        compiler_params=pltpu.CompilerParams(vmem_limit_bytes=56 * 1024 * 1024),
    )(*arrays)


def tables(ne, side):
    wide = 2 * side
    gp = min(4, wide)
    perm = np.zeros((gp * OUT, gp * OUT), np.float32)
    for j in range(4):
        for s in range(gp):
            for r in range(CAP):
                perm[j * gp * CAP + s * CAP + r, s * OUT + j * CAP + r] = 1.0
    back = np.zeros((2, wide * BACK, wide * CAP), np.float32)
    for s in range(wide):
        for r in range(CAP):
            for m in range(2):
                back[m, s * BACK + m * CAP + r, s * CAP + r] = 1.0
    expand = np.kron(np.eye(ne, dtype=np.float32), np.ones((1, BACK), np.float32))
    phase = np.tile(np.arange(BACK, dtype=np.float32), ne)[None, :]
    half = ml_dtypes.bfloat16
    return gp, perm.astype(half), back.astype(half), expand.astype(half), phase


def solution(mesh):
    ne, nt = mesh.shape["expert"], mesh.shape["tensor"]
    side = SIDE
    wide = 2 * side
    ny, half = ne // wide, nt // 2
    rows = ne * CAP
    ring = ring_chunks(ny)
    direct = ny - ring
    gp, perm, back, expand, phase = tables(ne, side)

    def step(tokens, cotangent, expert_ids, gate_probs, w_gate, w_up, w_down):
        owned, width = tokens.shape
        vmem = pl.BlockSpec(memory_space=pltpu.VMEM)
        hbm = pl.BlockSpec(memory_space=pl.ANY)
        dma = pltpu.SemaphoreType.DMA
        gi, gg, gu, gd = pl.pallas_call(
            functools.partial(kernel, ne, nt, side, gp),
            out_shape=(
                jax.ShapeDtypeStruct((owned, PART), BF),
                jax.ShapeDtypeStruct((width, LANES), BF),
                jax.ShapeDtypeStruct((width, LANES), BF),
                jax.ShapeDtypeStruct((LANES, width), BF),
            ),
            in_specs=[vmem] * 4 + [hbm] * 3 + [vmem] + [hbm] * 2 + [vmem],
            out_specs=(vmem,) * 4,
            scratch_shapes=[
                pltpu.VMEM((LANES, width), BF),
                pltpu.VMEM(back.shape, BF),
                pltpu.VMEM(expand.shape, BF),
                pltpu.VMEM((ne, owned), F32),
                pltpu.VMEM((ne, owned), F32),
                pltpu.VMEM((4 * owned, 2 * LANES), BF),
                pltpu.VMEM((4 * owned, nt * LANES), BF),
                pltpu.VMEM((wide * OUT, 4 * owned), BF),
                pltpu.VMEM((ring * wide * OUT, 2 * LANES), BF),
                pltpu.VMEM((ring * wide * OUT, 2 * LANES), BF),
                pltpu.VMEM((direct * wide * OUT, nt * LANES), BF),
                pltpu.VMEM((direct * wide * OUT, nt * LANES), BF),
                pltpu.VMEM((nt, rows, 2 * PART), BF),
                pltpu.VMEM((width, 2 * LANES), BF),
                pltpu.VMEM((rows, 2 * LANES), BF),
                pltpu.VMEM((rows, LANES), BF),
                pltpu.VMEM((2, half, rows, PART), BF),
                pltpu.VMEM((2, half, rows, PART), BF),
                pltpu.VMEM((ne * BACK, LANES), BF),
                pltpu.VMEM((ne * BACK, LANES), BF),
                pltpu.VMEM((owned, ne * BACK), BF),
                pltpu.VMEM((owned, ne * BACK), BF),
                dma,
                dma,
                dma((ny,)),
                dma((2, half - 1)),
                dma((2, half - 1, ring)),
                dma((2, half)),
                dma((2, half, ny)),
                dma,
                dma((ny,)),
                dma((5,)),
            ],
            compiler_params=pltpu.CompilerParams(
                collective_id=0, has_side_effects=True, vmem_limit_bytes=56 * 1024 * 1024
            ),
        )(
            expert_ids.T,
            gate_probs.T,
            tokens,
            cotangent,
            w_gate[0],
            w_up[0],
            w_down[0],
            jnp.asarray(perm),
            jnp.asarray(back),
            jnp.asarray(expand),
            jnp.asarray(phase),
        )
        gi, gg, gu, gd = settle(gi, gg, gu, gd)
        return gi, gg[None], gu[None], gd[None]

    return jax.shard_map(
        step,
        mesh=mesh,
        in_specs=(
            P("expert", None),
            P("expert", None),
            P("expert", None),
            P("expert", None),
            P("expert", None, "tensor"),
            P("expert", None, "tensor"),
            P("expert", "tensor", None),
        ),
        out_specs=(
            P("expert", "tensor"),
            P("expert", None, "tensor"),
            P("expert", None, "tensor"),
            P("expert", "tensor", None),
        ),
        check_vma=False,
    )
```
